128 devices in a mesh: grp: 4 (over y_hi, core), seq: 32 (over y_lo, x, z).
Axes of the slice: x: 4, y: 4 (y_hi: 2, y_lo: 2; y = y_hi * 2 + y_lo), z: 4, core: 2. Of those that a mesh axis runs over, the one named last changes fastest.
Arguments:
- queries: bfloat16 [65536, 1024], P(('grp', 'seq')), may hold values from -200 to 200
- keys: bfloat16 [65536, 1024], P(('grp', 'seq')), may hold values from -5 to 5
- values: bfloat16 [65536, 1024], P(('grp', 'seq')), may hold values from -6 to 6
- out_grad: bfloat16 [65536, 1024], P(('grp', 'seq')), may hold values from -6 to 6
Outputs:
- attended: bfloat16 [65536, 1024], P(('grp', 'seq'))
- grad_queries: bfloat16 [65536, 1024], P(('grp', 'seq'))
- grad_keys: bfloat16 [65536, 1024], P(('grp', 'seq'))
- grad_values: bfloat16 [65536, 1024], P(('grp', 'seq'))
The draws below stay inside these ranges and needn't reach their ends.
All inputs are finite; a program needn't handle non-finite values.
Results may differ from the reference program's by a relative error of at most 0.02.
Values may be sent and summed in bfloat16 or wider, within the bound.
No kernel may reach another device: no remote copies, remote signals or barrier semaphores. Data moves between devices by JAX's collectives and lax.ppermute only.
A program may use at most 128 MiB of HBM per device.

```python
import math
import jax
import jax.numpy as jnp
from jax import lax

D = 1024
H = 16
HD = 64
BLOCK = 512
P1 = 4
P2 = 32
RATIO = 8
FR_DEV = 512
FRAMES = 65536
NEAR = 128
GROUP_ROWS = 512
TOP_ROWS = 256
KEYS = 1536
N_SEQ = 32


def shared_base(key):
    base_rows = jnp.clip(jax.random.normal(key, (FRAMES, D), jnp.float32), -5.0, 5.0)
    return base_rows


def draw_keys(key, part):
    base_rows = shared_base(key)
    return base_rows.astype(jnp.bfloat16)


def draw_queries(key, part):
    key = jax.random.fold_in(key, 2)
    return jnp.clip(jax.random.normal(key, (FRAMES, D), jnp.float32), -5.0, 5.0).astype(jnp.bfloat16)


def block_levels(key, extent, cuts, smallest, high):
    loudness, own = 1.0, jax.random.fold_in(key, 6)
    for dim, shards_of in cuts:
        heights = jnp.exp(jax.random.uniform(jax.random.fold_in(own, dim), (shards_of,), jnp.float32, smallest / len(cuts), high / len(cuts)))
        loudness = loudness * jnp.repeat(heights, extent[dim] // shards_of).reshape([-1 if axis == dim else 1 for axis in range(len(extent))])
    return loudness


def normal_values(own_key, shape, width, most, shards=(), kind=jnp.bfloat16):
    values = width * jax.random.normal(own_key, shape, jnp.float32)
    if shards:
        values = values * block_levels(own_key, shape, shards, -0.22, 0.18)
    return jnp.clip(values, -most, most).astype(kind)


def setup_inputs(seed: int = 0) -> dict:
    seeds = jax.random.split(jax.random.key(seed), 5)
    queries = draw_queries(jax.random.fold_in(seeds[4], 71), 0)
    keys = draw_keys(jax.random.fold_in(seeds[4], 71), 0)
    values = normal_values(seeds[2], (FRAMES, D), 1.0, 6.0, ((0, 128),))
    out_grad = normal_values(seeds[3], (FRAMES, D), 1.0, 6.0, ((0, 128),))
    return {"queries": queries, "keys": keys, "values": values, "out_grad": out_grad}


EPS = 1e-06
NEG = -1e+30
HIGH = lax.Precision.HIGHEST

def keep_bf16(value):
    rounded = lax.optimization_barrier(value.astype(jnp.bfloat16)).astype(jnp.float32)
    return value + lax.stop_gradient(rounded - value)

def summarize(stacked, factor):
    count_rows = stacked.shape[1] // factor
    pooled = lax.optimization_barrier(jnp.mean(stacked.reshape(2, count_rows, factor, H, HD), axis=2))
    scaled = pooled * lax.rsqrt(lax.optimization_barrier(jnp.mean(pooled * pooled, axis=-1, keepdims=True)) + EPS)
    return keep_bf16(scaled.reshape(2, count_rows, H * HD))

def attend(query_rows, grad_rows, key_rows, value_rows, key_live):
    score_scale = 1.0 / math.sqrt(HD)
    qpart = query_rows.reshape(-1, H, HD)
    gpart = grad_rows.reshape(-1, H, HD)
    kpart = key_rows.reshape(-1, H, HD)
    vpart = value_rows.reshape(-1, H, HD)
    scores = jnp.einsum('qhd,khd->hqk', qpart, kpart, precision=HIGH) * score_scale
    scores = jnp.where(key_live[None, None, :], scores, NEG)
    largest = lax.optimization_barrier(jnp.max(scores, axis=-1, keepdims=True))
    unnormed = jnp.exp(scores - largest)
    attn_probs = unnormed / lax.optimization_barrier(jnp.sum(unnormed, axis=-1, keepdims=True))
    probs_low = lax.optimization_barrier(attn_probs.astype(jnp.bfloat16)).astype(jnp.float32)
    output = jnp.einsum('hqk,khd->qhd', probs_low, vpart, precision=HIGH)
    prob_grad = jnp.einsum('qhd,khd->hqk', gpart, vpart, precision=HIGH)
    row_delta = lax.optimization_barrier(jnp.sum(attn_probs * prob_grad, axis=-1, keepdims=True))
    score_grad = attn_probs * (prob_grad - row_delta) * score_scale
    score_grad = lax.optimization_barrier(score_grad.astype(jnp.bfloat16)).astype(jnp.float32)
    query_grad = jnp.einsum('hqk,khd->qhd', score_grad, kpart, precision=HIGH)
    key_grad = jnp.einsum('hqk,qhd->khd', score_grad, qpart, precision=HIGH)
    value_grad = jnp.einsum('hqk,qhd->khd', probs_low, gpart, precision=HIGH)
    return (output.reshape(-1, D), query_grad.reshape(-1, D), key_grad.reshape(-1, D), value_grad.reshape(-1, D))

def reference(queries, keys, values, out_grad):
    stacked_kv = jnp.stack([keys, values]).astype(jnp.float32)
    near_all, near_pull = jax.vjp(lambda t: summarize(t, P1), stacked_kv)
    group_all, group_pull = jax.vjp(lambda t: summarize(t, P2), stacked_kv)
    top_all, top_pull = jax.vjp(lambda t: summarize(t, RATIO), group_all)
    blocks = FRAMES // BLOCK
    group_blocks = FR_DEV * N_SEQ // BLOCK
    near_ext = jnp.pad(near_all, ((0, 0), (NEAR, NEAR), (0, 0)))
    query_full = queries.astype(jnp.float32)
    grad_full = out_grad.astype(jnp.float32)
    position = jnp.arange(KEYS, dtype=jnp.int32)
    in_before = jnp.logical_and(position >= BLOCK, position < BLOCK + NEAR)
    in_after = jnp.logical_and(position >= BLOCK + NEAR, position < BLOCK + 2 * NEAR)

    def step(totals, block_index):
        group_grad, top_grad = totals
        offset = block_index * BLOCK
        query_rows = lax.dynamic_slice_in_dim(query_full, offset, BLOCK, 0)
        grad_rows = lax.dynamic_slice_in_dim(grad_full, offset, BLOCK, 0)
        diagonal = lax.dynamic_slice_in_dim(stacked_kv, offset, BLOCK, 1)
        before_rows = lax.dynamic_slice_in_dim(near_ext, block_index * NEAR, NEAR, 1)
        after_rows = lax.dynamic_slice_in_dim(near_ext, (block_index + 2) * NEAR, NEAR, 1)
        member = block_index // group_blocks
        group_rows = lax.dynamic_slice_in_dim(group_all, member * GROUP_ROWS, GROUP_ROWS, 1)
        key_sets = jnp.concatenate([diagonal, before_rows, after_rows, group_rows, top_all], axis=1)
        key_live = jnp.logical_not(jnp.logical_or(jnp.logical_and(in_before, block_index == 0), jnp.logical_and(in_after, block_index == blocks - 1)))
        output, query_grad, key_grad, value_grad = attend(query_rows, grad_rows, key_sets[0], key_sets[1], key_live)
        pair_grad = jnp.stack([key_grad, value_grad])
        lower = BLOCK + 2 * NEAR
        old_group = lax.dynamic_slice_in_dim(group_grad, member * GROUP_ROWS, GROUP_ROWS, 1)
        group_grad = lax.dynamic_update_slice_in_dim(group_grad, old_group + pair_grad[:, lower:lower + GROUP_ROWS], member * GROUP_ROWS, 1)
        top_grad = top_grad + pair_grad[:, lower + GROUP_ROWS:]
        outs = (output.astype(jnp.bfloat16), query_grad.astype(jnp.bfloat16), pair_grad[:, :BLOCK], pair_grad[:, BLOCK:BLOCK + NEAR], pair_grad[:, BLOCK + NEAR:BLOCK + 2 * NEAR])
        return ((group_grad, top_grad), outs)
    start_totals = (jnp.zeros((2, FRAMES // P2, D), jnp.float32), jnp.zeros((2, TOP_ROWS, D), jnp.float32))
    (group_grad, top_grad), stacked_outs = lax.scan(step, start_totals, jnp.arange(blocks, dtype=jnp.int32))
    attended_blocks, query_blocks, diag_grads, before_grads, after_grads = stacked_outs
    zero_pad = jnp.zeros((2, 2, NEAR, D), jnp.float32)
    ext_grads = jnp.concatenate([before_grads, zero_pad]) + jnp.concatenate([zero_pad, after_grads])
    near_grad = jnp.moveaxis(ext_grads[1:blocks + 1], 1, 0).reshape(2, FRAMES // P1, D)
    group_total = group_grad + top_pull(top_grad)[0]
    diag_total = jnp.moveaxis(diag_grads, 1, 0).reshape(2, FRAMES, D)
    kv_grad = diag_total + near_pull(near_grad)[0] + group_pull(group_total)[0]
    return (attended_blocks.reshape(FRAMES, D), query_blocks.reshape(FRAMES, D), kv_grad[0].astype(jnp.bfloat16), kv_grad[1].astype(jnp.bfloat16))
```

```python
import math

import jax
import jax.numpy as jnp
from jax import lax
from jax.experimental import pallas as pl
from jax.experimental.pallas import tpu as pltpu
from jax.sharding import PartitionSpec as P

D = 1024
H = 16
HD = 64
PAIR = 2 * HD
BLOCK = 512
P1 = 4
P2 = 32
RATIO = 8
NEAR = BLOCK // P1
OWN = BLOCK // P2
N_SEQ = 32
GROUP = OWN * N_SEQ
TOP = 256
KEYS = BLOCK + 2 * NEAR + GROUP + TOP
CHUNK = 256

EPS = 1e-06
NEG = -1e30
LOG2E = math.log2(math.e)

F32 = jnp.float32
BF16 = jnp.bfloat16


def dot(a, b):
    return jnp.dot(a, b, preferred_element_type=F32)


def pieces(x, count):
    parts = []
    for _ in range(count):
        low = x.astype(BF16)
        parts.append(low)
        x = x - low.astype(F32)
    return parts


def pool_matrix(rows, cols, factor):
    row = lax.broadcasted_iota(jnp.int32, (rows, cols), 0)
    col = lax.broadcasted_iota(jnp.int32, (rows, cols), 1)
    return jnp.where(col // factor == row, 1.0, 0.0).astype(BF16)


def spread_matrix(rows, cols, factor):
    row = lax.broadcasted_iota(jnp.int32, (rows, cols), 0)
    col = lax.broadcasted_iota(jnp.int32, (rows, cols), 1)
    return jnp.where(row // factor == col, 1.0, 0.0).astype(BF16)


def head_means(x):
    width = 256
    row = lax.broadcasted_iota(jnp.int32, (width, width), 0)
    col = lax.broadcasted_iota(jnp.int32, (width, width), 1)
    same = jnp.where(row // HD == col // HD, 1.0, 0.0).astype(BF16)
    tiles = []
    for start in range(0, x.shape[1], width):
        tile = x[:, start : start + width]
        tiles.append(sum(dot(part, same) for part in pieces(tile, 3)))
    return jnp.concatenate(tiles, axis=1) * (1.0 / HD)


def normalize(pooled):
    return pooled * lax.rsqrt(head_means(pooled * pooled) + EPS)


def normalize_back(pooled, upstream):
    scale = lax.rsqrt(head_means(pooled * pooled) + EPS)
    inner = head_means(pooled * upstream)
    return scale * (upstream - pooled * (scale * scale * inner))


def top_pool(rows):
    return jnp.mean(rows.astype(F32).reshape(rows.shape[0] // RATIO, RATIO, rows.shape[1]), axis=1)


def summaries_kernel(k_ref, v_ref, near_ref, group_ref, top_ref):
    for index, ref in enumerate((k_ref, v_ref)):
        rows = ref[...]
        near = dot(pool_matrix(NEAR, BLOCK, P1), rows) * (1.0 / P1)
        near_ref[index] = normalize(near).astype(BF16)
        group = dot(pool_matrix(OWN, BLOCK, P2), rows) * (1.0 / P2)
        group = normalize(group).astype(BF16)
        group_ref[index] = group
        top_ref[index] = normalize(top_pool(group)).astype(BF16)


def summaries(keys, values):
    return pl.pallas_call(
        summaries_kernel,
        out_shape=(
            jax.ShapeDtypeStruct((2, NEAR, D), BF16),
            jax.ShapeDtypeStruct((2, OWN, D), BF16),
            jax.ShapeDtypeStruct((2, OWN // RATIO, D), BF16),
        ),
        compiler_params=pltpu.CompilerParams(vmem_limit_bytes=48 * 1024 * 1024),
        name="summaries",
    )(keys, values)


def finish_kernel(k_ref, v_ref, diag_ref, prev_ref, next_ref, group_ref, top_ref, dk_ref, dv_ref):
    for index, (ref, out_ref) in enumerate(((k_ref, dk_ref), (v_ref, dv_ref))):
        rows = ref[...]
        near = dot(pool_matrix(NEAR, BLOCK, P1), rows) * (1.0 / P1)
        near_up = prev_ref[index].astype(F32) + next_ref[index].astype(F32)
        near_back = normalize_back(near, near_up) * (1.0 / P1)
        group = dot(pool_matrix(OWN, BLOCK, P2), rows) * (1.0 / P2)
        group_low = normalize(group).astype(BF16)
        top_back = normalize_back(top_pool(group_low), top_ref[index]) * (1.0 / RATIO)
        top_back = jnp.broadcast_to(top_back[:, None, :], (OWN // RATIO, RATIO, D)).reshape(OWN, D)
        group_back = normalize_back(group, group_ref[index] + top_back) * (1.0 / P2)
        total = diag_ref[index]
        for part in pieces(near_back, 2):
            total = total + dot(spread_matrix(BLOCK, NEAR, P1), part)
        for part in pieces(group_back, 2):
            total = total + dot(spread_matrix(BLOCK, OWN, P2), part)
        out_ref[...] = total.astype(BF16)


def finish(keys, values, diag, from_prev, from_next, group, top):
    return pl.pallas_call(
        finish_kernel,
        out_shape=(
            jax.ShapeDtypeStruct((BLOCK, D), BF16),
            jax.ShapeDtypeStruct((BLOCK, D), BF16),
        ),
        compiler_params=pltpu.CompilerParams(vmem_limit_bytes=56 * 1024 * 1024),
        name="finish",
    )(keys, values, diag, from_prev, from_next, group, top)


def attend_kernel(
    live_ref, q_ref, g_ref, k_ref, v_ref, before_ref, after_ref, group_ref, top_ref,
    out_ref, dq_ref, diag_ref, dbefore_ref, dafter_ref, dgroup_ref, dtop_ref,
    kcat, vcat, scores, weights, sgrad,
):
    for index, (cat, own) in enumerate(((kcat, k_ref), (vcat, v_ref))):
        cat[0:BLOCK] = own[...]
        cat[BLOCK : BLOCK + NEAR] = before_ref[index]
        cat[BLOCK + NEAR : BLOCK + 2 * NEAR] = after_ref[index]
        low = BLOCK + 2 * NEAR
        cat[low : low + GROUP] = group_ref[:, index].reshape(GROUP, PAIR)
        cat[low + GROUP :] = top_ref[index]
    queries = q_ref[...]
    q_t = queries.T
    g_t = g_ref[...].T
    v_t = vcat[...].T
    k_t = kcat[...].T
    zeros_t = jnp.zeros((HD, BLOCK), BF16)
    ones_t = jnp.ones((HD, KEYS), BF16)
    chunks = range(0, KEYS, CHUNK)
    lane = lax.broadcasted_iota(jnp.int32, (CHUNK, PAIR), 1)
    near_row = lax.broadcasted_iota(jnp.int32, (CHUNK, 1), 0)
    near_bias = jnp.where(near_row < NEAR, live_ref[0], live_ref[1])
    row64 = lax.broadcasted_iota(jnp.int32, (HD, BLOCK), 0)

    def around(head, mine, other):
        return jnp.concatenate([mine, other] if head == 0 else [other, mine], axis=0)

    out_t, dq_t, gs_t = [], [], []
    for head in range(2):
        cut = slice(head * HD, head * HD + HD)
        mine = (lane < HD) if head == 0 else (lane >= HD)
        q_head = around(head, q_t[cut], zeros_t)
        largest = None
        for start in chunks:
            part = dot(kcat[start : start + CHUNK], q_head)
            if start == BLOCK:
                part = part + near_bias
            scores[start : start + CHUNK] = part
            top = jnp.max(part.reshape(CHUNK // 8, 8, BLOCK), axis=0)
            largest = top if largest is None else jnp.maximum(largest, top)
        largest = jnp.max(largest, axis=0, keepdims=True)
        for start in chunks:
            part = (scores[start : start + CHUNK] - largest) * (LOG2E / math.sqrt(HD))
            weights[head, start : start + CHUNK] = jnp.exp2(part).astype(BF16)
        v_head = around(head, v_t[cut], ones_t)
        both = dot(v_head, weights[head])
        other = HD if head == 0 else 0
        inverse = 1.0 / both[other : other + 1]
        attended = both[cut] * inverse
        out_t.append(attended)
        scaled = (g_t[cut].astype(F32) * inverse).astype(BF16)
        gs_t.append(scaled)
        delta = jnp.sum(scaled.astype(F32) * attended, axis=0, keepdims=True)
        extra = jnp.zeros((HD, BLOCK), F32)
        for place, piece in enumerate(pieces(-delta, 3)):
            extra = jnp.where(row64 == place, piece.astype(F32), extra)
        g_head = around(head, scaled, extra.astype(BF16))
        for start in chunks:
            v_part = jnp.where(mine, vcat[start : start + CHUNK], jnp.ones((), BF16))
            part = dot(v_part, g_head)
            part = part * weights[head, start : start + CHUNK].astype(F32)
            sgrad[head, start : start + CHUNK] = part.astype(BF16)
        dq_t.append(dot(k_t, sgrad[head])[cut])
    out_ref[...] = jnp.concatenate(out_t, axis=0).T.astype(BF16)
    dq_ref[...] = (jnp.concatenate(dq_t, axis=0).T * (1.0 / math.sqrt(HD))).astype(BF16)
    scaled = jnp.concatenate(gs_t, axis=0).T
    qlane = lax.broadcasted_iota(jnp.int32, (BLOCK, PAIR), 1)
    zero = jnp.zeros((), BF16)
    q_low, q_high = jnp.where(qlane < HD, queries, zero), jnp.where(qlane < HD, zero, queries)
    g_low, g_high = jnp.where(qlane < HD, scaled, zero), jnp.where(qlane < HD, zero, scaled)
    for start in chunks:
        cut = slice(start, start + CHUNK)
        dk = (dot(sgrad[0, cut], q_low) + dot(sgrad[1, cut], q_high)) * (1.0 / math.sqrt(HD))
        dv = dot(weights[0, cut], g_low) + dot(weights[1, cut], g_high)
        for index, value in enumerate((dk, dv)):
            if start < BLOCK:
                diag_ref[index, cut] = value
            elif start < BLOCK + 2 * NEAR:
                dbefore_ref[index] = value[:NEAR].astype(BF16)
                dafter_ref[index] = value[NEAR:].astype(BF16)
            elif start < BLOCK + 2 * NEAR + GROUP:
                at = (start - BLOCK - 2 * NEAR) // OWN
                dgroup_ref[at : at + CHUNK // OWN, index] = value.astype(BF16).reshape(
                    CHUNK // OWN, OWN, PAIR
                )
            else:
                dtop_ref[index] = value.astype(BF16)


def attend(live, queries, out_grad, keys, values, before, after, group, top):
    def rows(count):
        return pl.BlockSpec((count, PAIR), lambda p: (0, p))

    def stacked(count):
        return pl.BlockSpec((2, count, PAIR), lambda p: (0, 0, p))

    spread = pl.BlockSpec((N_SEQ, 2, OWN, PAIR), lambda p: (0, 0, 0, p))
    return pl.pallas_call(
        attend_kernel,
        grid=(H // 2,),
        in_specs=[pl.BlockSpec(memory_space=pltpu.SMEM)]
        + [rows(BLOCK)] * 4
        + [stacked(NEAR)] * 2
        + [spread, stacked(TOP)],
        out_specs=[rows(BLOCK)] * 2 + [stacked(BLOCK)] + [stacked(NEAR)] * 2 + [spread, stacked(TOP)],
        out_shape=(
            jax.ShapeDtypeStruct((BLOCK, D), BF16),
            jax.ShapeDtypeStruct((BLOCK, D), BF16),
            jax.ShapeDtypeStruct((2, BLOCK, D), F32),
            jax.ShapeDtypeStruct((2, NEAR, D), BF16),
            jax.ShapeDtypeStruct((2, NEAR, D), BF16),
            jax.ShapeDtypeStruct((N_SEQ, 2, OWN, D), BF16),
            jax.ShapeDtypeStruct((2, TOP, D), BF16),
        ),
        scratch_shapes=[
            pltpu.VMEM((KEYS, PAIR), BF16),
            pltpu.VMEM((KEYS, PAIR), BF16),
            pltpu.VMEM((KEYS, BLOCK), F32),
            pltpu.VMEM((2, KEYS, BLOCK), BF16),
            pltpu.VMEM((2, KEYS, BLOCK), BF16),
        ],
        compiler_params=pltpu.CompilerParams(vmem_limit_bytes=56 * 1024 * 1024),
        name="attend",
    )(live, queries, out_grad, keys, values, before, after, group, top)


def shifted(block, distance):
    count = lax.axis_size(("grp", "seq"))
    route = [(i, i + distance) for i in range(count) if 0 <= i + distance < count]
    return lax.ppermute(block, ("grp", "seq"), route)


def grp_swap(block, bit):
    return lax.ppermute(block, "grp", [(i, i ^ bit) for i in range(4)])


def per_device(queries, keys, values, out_grad):
    device = lax.axis_index("grp") * N_SEQ + lax.axis_index("seq")
    count = lax.axis_size(("grp", "seq"))
    near, group, top = summaries(keys, values)
    before = shifted(near, 1)
    after = shifted(near, -1)
    top_pair = jnp.stack([top, grp_swap(top, 2)], axis=1)
    payload = jnp.concatenate([group.reshape(2 * OWN, D), top_pair.reshape(8, D)], axis=0)
    everyone = jnp.broadcast_to(payload[None], (N_SEQ,) + payload.shape)
    everyone = lax.all_to_all(everyone, "seq", 0, 0, tiled=True)
    group_all = everyone[:, : 2 * OWN].reshape(N_SEQ, 2, OWN, D)
    top_mine = everyone[:, 2 * OWN :]
    top_other = grp_swap(top_mine, 1)
    top_all = jnp.stack([top_mine, top_other]).reshape(2, N_SEQ, 2, 4, D)
    top_all = top_all.transpose(2, 0, 1, 3, 4).reshape(2, TOP, D)
    live = jnp.stack(
        [jnp.where(device == 0, NEG, 0.0), jnp.where(device == count - 1, NEG, 0.0)]
    ).astype(F32)
    out, dq, diag, dbefore, dafter, dgroup, dtop = attend(
        live, queries, out_grad, keys, values, before, after, group_all, top_all
    )
    from_next = shifted(dbefore, -1)
    from_prev = shifted(dafter, 1)
    dtop = dtop.reshape(2, 2, N_SEQ, 4, D).transpose(1, 2, 0, 3, 4).reshape(2, N_SEQ, 8, D)
    dtop_mine = (dtop[0].astype(F32) + grp_swap(dtop[1], 1).astype(F32)).astype(BF16)
    returned = jnp.concatenate([dgroup.reshape(N_SEQ, 2 * OWN, D), dtop_mine], axis=1)
    returned = lax.all_to_all(returned, "seq", 0, 0, tiled=True)
    summed = jnp.sum(returned.astype(F32), axis=0)
    group_up = summed[: 2 * OWN].reshape(2, OWN, D)
    top_up = summed[2 * OWN :].reshape(2, 2, 2, D)
    top_up = top_up[:, 0] + grp_swap(top_up[:, 1], 2)
    dk, dv = finish(keys, values, diag, from_prev, from_next, group_up, top_up)
    return out, dq, dk, dv


def solution(mesh):
    spec = P(("grp", "seq"), None)
    return jax.shard_map(
        per_device, mesh=mesh, in_specs=(spec,) * 4, out_specs=(spec,) * 4, check_vma=False
    )
```

```python
import math

import jax
import jax.numpy as jnp
from jax import lax
from jax.experimental import pallas as pl
from jax.experimental.pallas import tpu as pltpu
from jax.sharding import PartitionSpec as P

D = 1024
H = 16
HD = 64
PAIR = 2 * HD
PAIRS = D // PAIR
BLOCK = 512
BOTH = 2 * BLOCK
P1 = 4
P2 = 32
RATIO = 8
NEAR = BLOCK // P1
OWN = BLOCK // P2
N_SEQ = 32
GROUP = OWN * N_SEQ
TOP = 256
SENT = 2 * OWN + 8
WIDE = GROUP + TOP + 2 * NEAR
CHUNK = 256
ROWS = 128
TILES = BLOCK // ROWS
UNROLL = 2
SOFT = 1.0 / math.sqrt(HD)

EPS = 1e-06
NEG = -1e30
LOG2E = math.log2(math.e)

F32 = jnp.float32
BF16 = jnp.bfloat16


def dot(a, b):
    return jnp.dot(a, b, preferred_element_type=F32)


def pieces(x, count):
    parts = []
    for _ in range(count):
        low = x.astype(BF16)
        parts.append(low)
        x = x - low.astype(F32)
    return parts


def pool_matrix(rows, cols, factor):
    row = lax.broadcasted_iota(jnp.int32, (rows, cols), 0)
    col = lax.broadcasted_iota(jnp.int32, (rows, cols), 1)
    return jnp.where(col // factor == row, 1.0, 0.0).astype(BF16)


def spread_matrix(rows, cols, factor):
    row = lax.broadcasted_iota(jnp.int32, (rows, cols), 0)
    col = lax.broadcasted_iota(jnp.int32, (rows, cols), 1)
    return jnp.where(row // factor == col, 1.0, 0.0).astype(BF16)


def head_means(*xs):
    width = 256
    row = lax.broadcasted_iota(jnp.int32, (width, width), 0)
    col = lax.broadcasted_iota(jnp.int32, (width, width), 1)
    same = jnp.where(row // HD == col // HD, 1.0 / HD, 0.0).astype(BF16)
    stack = [x[:, start : start + width] for x in xs for start in range(0, D, width)]
    stack = jnp.concatenate(stack, axis=0)
    count = stack.shape[0]
    found = dot(jnp.concatenate(pieces(stack, 3), axis=0), same)
    found = found[:count] + found[count : 2 * count] + found[2 * count :]
    means, at = [], 0
    for x in xs:
        rows = x.shape[0]
        tiles = [found[at + t * rows : at + t * rows + rows] for t in range(D // width)]
        means.append(jnp.concatenate(tiles, axis=1))
        at += rows * (D // width)
    return means


def normalize(*pooled):
    means = head_means(*[x * x for x in pooled])
    return [x * lax.rsqrt(mean + EPS) for x, mean in zip(pooled, means)]


def normalize_back(pooled, upstream):
    means = head_means(*[x * x for x in pooled], *[x * up for x, up in zip(pooled, upstream)])
    back = []
    for x, up, mean, inner in zip(pooled, upstream, means, means[len(pooled) :]):
        scale = lax.rsqrt(mean + EPS)
        back.append(scale * (up - x * (scale * scale * inner)))
    return back


def top_pool(rows):
    return jnp.mean(rows.astype(F32).reshape(rows.shape[0] // RATIO, RATIO, rows.shape[1]), axis=1)


def summaries_kernel(
    k_ref, v_ref, near_ref, near_pooled_ref, top_ref, pooled_ref, payload_ref, groups
):
    tile = pl.program_id(0)
    pooled = []
    for index, ref in enumerate((k_ref, v_ref)):
        rows = ref[...]
        pooled.append(dot(pool_matrix(ROWS // P1, ROWS, P1), rows) * (1.0 / P1))
        near_pooled_ref[index] = pooled[index]
        groups[index, tile] = dot(pool_matrix(8, ROWS, P2), rows) * (1.0 / P2)
    for index, near in enumerate(normalize(*pooled)):
        near_ref[index] = near.astype(BF16)

    @pl.when(tile == TILES - 1)
    def _():
        pooled = []
        for index in range(2):
            parts = [groups[index, t][: ROWS // P2] for t in range(TILES)]
            pooled.append(jnp.concatenate(parts, axis=0))
            pooled_ref[index] = pooled[index]
        low = [group.astype(BF16) for group in normalize(*pooled)]
        for index, group in enumerate(low):
            payload_ref[:, index * OWN : index * OWN + OWN] = jnp.broadcast_to(
                group[None], (N_SEQ, OWN, D)
            )
        for index, top in enumerate(normalize(*[top_pool(group) for group in low])):
            top_ref[index] = top.astype(BF16)


def collect_kernel(back_ref, up_ref, top_ref):
    up_ref[...] = jnp.sum(back_ref[:, : 2 * OWN].astype(F32), axis=0).reshape(2, OWN, D)
    top_ref[...] = jnp.sum(back_ref[:, 2 * OWN :].astype(F32), axis=0)


def finish_kernel(
    diag_ref, near_pooled_ref, prev_ref, next_ref, pooled_ref, up_ref, top_ref, swapped_ref,
    dk_ref, dv_ref, spread,
):
    tile = pl.program_id(0)

    @pl.when(tile == 0)
    def _():
        pooled = [pooled_ref[0], pooled_ref[1]]
        tops = [top_pool(group.astype(BF16)) for group in normalize(*pooled)]
        top_up = [
            top_ref[4 * index : 4 * index + 2] + swapped_ref[4 * index + 2 : 4 * index + 4]
            for index in range(2)
        ]
        ups = []
        for index, back in enumerate(normalize_back(tops, top_up)):
            back = jnp.broadcast_to(back[:, None, :] * (1.0 / RATIO), (OWN // RATIO, RATIO, D))
            ups.append(up_ref[index] + back.reshape(OWN, D))
        for index, back in enumerate(normalize_back(pooled, ups)):
            spread[index] = back * (1.0 / P2)

    count = ROWS // P1
    near_up = [prev_ref[index].astype(F32) + next_ref[index].astype(F32) for index in range(2)]
    near_back = normalize_back([near_pooled_ref[0], near_pooled_ref[1]], near_up)
    for index, out_ref in enumerate((dk_ref, dv_ref)):
        total = diag_ref[index]
        for part in pieces(near_back[index] * (1.0 / P1), 2):
            total = total + dot(spread_matrix(ROWS, count, P1), part)
        for place in range(ROWS // P2):
            cut = slice(place * P2, place * P2 + P2)
            row = spread[index, pl.ds(tile * (ROWS // P2) + place, 1)]
            out_ref[cut] = (total[cut] + row).astype(BF16)


def starts(count):
    return range(0, count, CHUNK)


def apart(x_t):
    zero = jnp.zeros((HD, BLOCK), x_t.dtype)
    first = jnp.concatenate([x_t[:HD], zero], axis=1)
    second = jnp.concatenate([zero, x_t[HD:]], axis=1)
    return jnp.concatenate([first, second], axis=0)


def together(x):
    return jnp.concatenate([x[:HD, :BLOCK], x[HD:PAIR, BLOCK:]], axis=0)


def by_head(row):
    return jnp.concatenate(
        [jnp.broadcast_to(row[:, :BLOCK], (HD, BLOCK)), jnp.broadcast_to(row[:, BLOCK:], (HD, BLOCK))],
        axis=0,
    )


def head_sums(x):
    return jnp.concatenate(
        [jnp.sum(x[:HD], axis=0, keepdims=True), jnp.sum(x[HD:], axis=0, keepdims=True)], axis=1
    )


def head_rows(x):
    lane = lax.broadcasted_iota(jnp.int32, x.shape, 1)
    zero = jnp.zeros((), BF16)
    return jnp.concatenate([jnp.where(lane < HD, x, zero), jnp.where(lane < HD, zero, x)], axis=0)


def forward(q_t, kcat, v_t, scores, weights, bias):
    count = kcat.shape[0]
    q_both = apart(q_t)
    largest = None
    for start in starts(count):
        part = dot(kcat[start : start + CHUNK], q_both)
        if start in bias:
            part = part + bias[start]
        scores[start : start + CHUNK] = part
        part = jnp.max(part.reshape(CHUNK // 8, 8, BOTH), axis=0)
        largest = part if largest is None else jnp.maximum(largest, part)
    largest = jnp.max(largest, axis=0, keepdims=True)
    for start in starts(count):
        part = (scores[start : start + CHUNK] - largest) * (LOG2E * SOFT)
        weights[start : start + CHUNK] = jnp.exp2(part).astype(BF16)
    found = dot(jnp.concatenate([v_t, jnp.ones((16, count), BF16)], axis=0), weights[...])
    return largest, found[PAIR : PAIR + 1], together(found)


def score_grads(scaled, delta, vones, weights, sgrad):
    row = lax.broadcasted_iota(jnp.int32, (16, BOTH), 0)
    extra = jnp.zeros((16, BOTH), F32)
    for place, piece in enumerate(pieces(-delta, 3)):
        extra = jnp.where(row == place, piece.astype(F32), extra)
    zero = jnp.zeros((PAIR - 16, BOTH), BF16)
    g_both = jnp.concatenate([apart(scaled), extra.astype(BF16), zero], axis=0)
    for start in starts(vones.shape[0]):
        cut = slice(start, start + CHUNK)
        part = dot(vones[cut], g_both)
        sgrad[cut] = (part * weights[cut].astype(F32)).astype(BF16)


def diag_kernel(q_ref, k_ref, v_ref, weights_ref, sum_ref, stats_ref, scores):
    largest, total, summed = forward(
        q_ref[...].T, k_ref, v_ref[...].T, scores, weights_ref.at[0], {}
    )
    stats_ref[0, 0:1] = largest
    stats_ref[0, 1:2] = total
    sum_ref[...] = summed


def low_rows(shape):
    return lax.broadcasted_iota(jnp.int32, shape, 1) < 4


def split_top(ref, lanes):
    both = ref[:, :, lanes].astype(F32).reshape(N_SEQ // 2, 2, 8, PAIR)
    first, second = both[:, 0], both[:, 1]
    low = low_rows(first.shape)
    k = jnp.where(low, first, pltpu.roll(second, 4, 1))
    v = jnp.where(low, pltpu.roll(first, 4, 1), second)
    return k.reshape(TOP // 2, PAIR).astype(BF16), v.reshape(TOP // 2, PAIR).astype(BF16)


def join_top(k, v):
    k = k.reshape(N_SEQ // 2, 8, PAIR)
    v = v.reshape(N_SEQ // 2, 8, PAIR)
    low = low_rows(k.shape)
    first = jnp.where(low, k, pltpu.roll(v, 4, 1))
    second = jnp.where(low, pltpu.roll(k, 4, 1), v)
    return jnp.stack([first, second], axis=1).reshape(N_SEQ, 8, PAIR).astype(BF16)


def wide_kernel(
    live_ref, q_ref, g_ref, before_ref, after_ref, sum_ref, stats_ref,
    group_ref, mine_ref, other_ref,
    out_ref, scaled_ref, delta_ref, kcat_ref, sgrad_ref,
    dgroup_ref, dmine_ref, dother_ref, dbefore_ref, dafter_ref,
    vones, scores, weights,
):
    near_row = lax.broadcasted_iota(jnp.int32, (CHUNK, 1), 0)
    bias = {GROUP + TOP: jnp.where(near_row < NEAR, live_ref[0], live_ref[1])}

    @pl.when(pl.program_id(0) == 0)
    def _():
        vones[:, :, PAIR:] = jnp.ones((UNROLL, WIDE, PAIR), BF16)

    for p in range(UNROLL):
        lanes = slice(p * PAIR, p * PAIR + PAIR)
        wide_pair(
            bias, q_ref.at[:, lanes], g_ref.at[:, lanes],
            before_ref.at[:, :, lanes], after_ref.at[:, :, lanes],
            sum_ref.at[lanes], stats_ref.at[p], group_ref.at[:, :, lanes],
            split_top(mine_ref, lanes), split_top(other_ref, lanes),
            out_ref.at[lanes], scaled_ref.at[lanes], delta_ref.at[p],
            kcat_ref.at[p], sgrad_ref.at[p],
            dgroup_ref.at[:, :, lanes], dmine_ref.at[:, :, lanes], dother_ref.at[:, :, lanes],
            dbefore_ref.at[:, :, lanes], dafter_ref.at[:, :, lanes],
            vones.at[p], scores.at[p], weights.at[p],
        )


def wide_pair(
    bias, q_ref, g_ref, before_ref, after_ref, sum_ref, stats_ref, group_ref, mine, other,
    out_ref, scaled_ref, delta_ref, kcat, sgrad,
    dgroup_ref, dmine_ref, dother_ref, dbefore_ref, dafter_ref,
    vones, scores, weights,
):
    kcat[0:GROUP] = group_ref[:, 0:OWN].reshape(GROUP, PAIR)
    vones[0:GROUP, :PAIR] = group_ref[:, OWN : 2 * OWN].reshape(GROUP, PAIR)
    for start, (k, v) in ((GROUP, mine), (GROUP + TOP // 2, other)):
        kcat[start : start + TOP // 2] = k
        vones[start : start + TOP // 2, :PAIR] = v
    for start, ref in ((GROUP + TOP, before_ref), (GROUP + TOP + NEAR, after_ref)):
        kcat[start : start + NEAR] = ref[0]
        vones[start : start + NEAR, :PAIR] = ref[1]
    queries = q_ref[...]
    largest, total, summed = forward(
        queries.T, kcat, vones[:, :PAIR].T, scores, weights, bias
    )
    local_largest, local_total = stats_ref[0:1], stats_ref[1:2]
    most = jnp.maximum(largest, local_largest)
    share = jnp.exp2((largest - most) * (LOG2E * SOFT))
    local_share = jnp.exp2((local_largest - most) * (LOG2E * SOFT))
    inverse = 1.0 / (share * total + local_share * local_total)
    share = by_head(share * inverse)
    local_share = by_head(local_share * inverse)
    attended = share * summed + local_share * sum_ref[...]
    out_ref[...] = attended.astype(BF16)
    grad = g_ref[...].T.astype(F32)
    local_scaled = (grad * local_share).astype(BF16)
    scaled_ref[...] = local_scaled
    delta_ref[0:1] = head_sums(local_scaled.astype(F32) * attended)
    scaled = (grad * share).astype(BF16)
    score_grads(scaled, head_sums(scaled.astype(F32) * attended), vones, weights, sgrad)
    q_rows = head_rows(queries)
    g_rows = head_rows(scaled.T)
    for start in starts(WIDE):
        cut = slice(start, start + CHUNK)
        dk = dot(sgrad[cut], q_rows) * SOFT
        dv = dot(weights[cut], g_rows)
        if start < GROUP:
            devices = slice(start // OWN, (start + CHUNK) // OWN)
            shape = (CHUNK // OWN, OWN, PAIR)
            dgroup_ref[devices, 0:OWN] = dk.astype(BF16).reshape(shape)
            dgroup_ref[devices, OWN : 2 * OWN] = dv.astype(BF16).reshape(shape)
        elif start < GROUP + TOP:
            half = TOP // 2
            dmine_ref[...] = join_top(dk[:half], dv[:half])
            dother_ref[...] = join_top(dk[half:], dv[half:])
        else:
            for index, value in enumerate((dk, dv)):
                dbefore_ref[index] = value[:NEAR].astype(BF16)
                dafter_ref[index] = value[NEAR:].astype(BF16)


def diag_back_kernel(
    q_ref, k_ref, v_ref, weights_ref, out_t_ref, scaled_ref, delta_ref, kcat_ref, wide_ref,
    out_ref, dq_ref, diag_ref, vones, sgrad,
):
    @pl.when(pl.program_id(0) == 0)
    def _():
        vones[:, PAIR:] = jnp.ones((BLOCK, PAIR), BF16)

    vones[:, :PAIR] = v_ref[...]
    out_ref[...] = out_t_ref[...].T
    weights = weights_ref.at[0]
    scaled = scaled_ref[...]
    score_grads(scaled, delta_ref[0, 0:1], vones, weights, sgrad)
    dq = dot(kcat_ref[0].T, wide_ref[0]) + dot(k_ref[...].T, sgrad[...])
    dq_ref[...] = (together(dq).T * SOFT).astype(BF16)
    q_rows = head_rows(q_ref[...])
    g_rows = head_rows(scaled.T)
    for start in starts(BLOCK):
        cut = slice(start, start + CHUNK)
        diag_ref[0, cut] = dot(sgrad[cut], q_rows) * SOFT
        diag_ref[1, cut] = dot(weights[cut], g_rows)


def shape_of(dtype, *shape):
    return jax.ShapeDtypeStruct(shape, dtype)


def on_lanes(*lead):
    return pl.BlockSpec(lead + (PAIR,), lambda p: (0,) * len(lead) + (p,))


def on_rows(*shape):
    return pl.BlockSpec(shape, lambda p: (p,) + (0,) * (len(shape) - 1))


def on_middle(*shape):
    return pl.BlockSpec(shape, lambda p: (0, p, 0))


def every(*shape):
    return pl.BlockSpec(shape, lambda p: (0,) * len(shape))


SMEM = pl.BlockSpec(memory_space=pltpu.SMEM)
SEQUENCE = on_lanes(BLOCK)
COLUMNS = on_rows(PAIR, BLOCK)
STATS = on_rows(1, 8, BOTH)
DIAG = on_rows(1, BLOCK, BOTH)
WIDE_KEYS = on_rows(1, WIDE, PAIR)
WIDE_GRADS = on_rows(1, WIDE, BOTH)


def call(kernel, name, steps, in_specs, out_specs, out_shape, scratch=()):
    return pl.pallas_call(
        kernel,
        grid=(steps,),
        in_specs=in_specs,
        out_specs=out_specs,
        out_shape=out_shape,
        scratch_shapes=scratch,
        compiler_params=pltpu.CompilerParams(vmem_limit_bytes=56 * 1024 * 1024),
        name=name,
    )


summaries = call(
    summaries_kernel,
    "summaries",
    TILES,
    [on_rows(ROWS, D)] * 2,
    [on_middle(2, ROWS // P1, D)] * 2
    + [every(2, OWN // RATIO, D), every(2, OWN, D), every(N_SEQ, 2 * OWN, D)],
    (
        shape_of(BF16, 2, NEAR, D),
        shape_of(F32, 2, NEAR, D),
        shape_of(BF16, 2, OWN // RATIO, D),
        shape_of(F32, 2, OWN, D),
        shape_of(BF16, N_SEQ, SENT, D),
    ),
    [pltpu.VMEM((2, TILES, 8, D), F32)],
)
diag_forward = call(
    diag_kernel,
    "diag_forward",
    PAIRS,
    [SEQUENCE] * 3,
    [DIAG, COLUMNS, STATS],
    (
        shape_of(BF16, PAIRS, BLOCK, BOTH),
        shape_of(F32, D, BLOCK),
        shape_of(F32, PAIRS, 8, BOTH),
    ),
    [pltpu.VMEM((BLOCK, BOTH), F32)],
)
def wide_lanes(*lead):
    return pl.BlockSpec(lead + (UNROLL * PAIR,), lambda p: (0,) * len(lead) + (p,))


wide_attend = call(
    wide_kernel,
    "wide_attend",
    PAIRS // UNROLL,
    [SMEM]
    + [wide_lanes(BLOCK)] * 2
    + [wide_lanes(2, NEAR)] * 2
    + [on_rows(UNROLL * PAIR, BLOCK), on_rows(UNROLL, 8, BOTH)]
    + [wide_lanes(N_SEQ, 2 * OWN)]
    + [wide_lanes(N_SEQ, 8)] * 2,
    [on_rows(UNROLL * PAIR, BLOCK)] * 2
    + [on_rows(UNROLL, 8, BOTH), on_rows(UNROLL, WIDE, PAIR), on_rows(UNROLL, WIDE, BOTH)]
    + [wide_lanes(N_SEQ, 2 * OWN)]
    + [wide_lanes(N_SEQ, 8)] * 2
    + [wide_lanes(2, NEAR)] * 2,
    (
        shape_of(BF16, D, BLOCK),
        shape_of(BF16, D, BLOCK),
        shape_of(F32, PAIRS, 8, BOTH),
        shape_of(BF16, PAIRS, WIDE, PAIR),
        shape_of(BF16, PAIRS, WIDE, BOTH),
        shape_of(BF16, N_SEQ, SENT, D),
        shape_of(BF16, N_SEQ, 8, D),
        shape_of(BF16, N_SEQ, 8, D),
        shape_of(BF16, 2, NEAR, D),
        shape_of(BF16, 2, NEAR, D),
    ),
    [
        pltpu.VMEM((UNROLL, WIDE, 2 * PAIR), BF16),
        pltpu.VMEM((UNROLL, WIDE, BOTH), F32),
        pltpu.VMEM((UNROLL, WIDE, BOTH), BF16),
    ],
)
diag_backward = call(
    diag_back_kernel,
    "diag_backward",
    PAIRS,
    [SEQUENCE] * 3 + [DIAG] + [COLUMNS] * 2 + [STATS, WIDE_KEYS, WIDE_GRADS],
    [SEQUENCE, SEQUENCE, on_lanes(2, BLOCK)],
    (shape_of(BF16, BLOCK, D), shape_of(BF16, BLOCK, D), shape_of(F32, 2, BLOCK, D)),
    [pltpu.VMEM((BLOCK, 2 * PAIR), BF16), pltpu.VMEM((BLOCK, BOTH), BF16)],
)
collect = pl.pallas_call(
    collect_kernel,
    out_shape=(shape_of(F32, 2, OWN, D), shape_of(F32, 8, D)),
    compiler_params=pltpu.CompilerParams(vmem_limit_bytes=16 * 1024 * 1024),
    name="collect",
)
finish = call(
    finish_kernel,
    "finish",
    TILES,
    [on_middle(2, ROWS, D)]
    + [on_middle(2, ROWS // P1, D)] * 3
    + [every(2, OWN, D)] * 2
    + [every(8, D)] * 2,
    [on_rows(ROWS, D)] * 2,
    (shape_of(BF16, BLOCK, D), shape_of(BF16, BLOCK, D)),
    [pltpu.VMEM((2, OWN, D), F32)],
)


def shifted(block, distance):
    count = lax.axis_size(("grp", "seq"))
    route = [(i, i + distance) for i in range(count) if 0 <= i + distance < count]
    return lax.ppermute(block, ("grp", "seq"), route)


def grp_swap(block, bit):
    return lax.ppermute(block, "grp", [(i, i ^ bit) for i in range(4)])


def per_device(queries, keys, values, out_grad):
    device = lax.axis_index("grp") * N_SEQ + lax.axis_index("seq")
    count = lax.axis_size(("grp", "seq"))
    live = jnp.stack(
        [jnp.where(device == 0, NEG, 0.0), jnp.where(device == count - 1, NEG, 0.0)]
    ).astype(F32)
    near, near_pooled, top, pooled, payload = summaries(keys, values)
    top_pair = jnp.stack([top, grp_swap(top, 2)], axis=1).reshape(8, D)
    tops = jnp.broadcast_to(top_pair[None], (N_SEQ, 8, D))
    payload = lax.dynamic_update_slice(payload, tops, (0, 2 * OWN, 0))
    everyone = lax.all_to_all(payload, "seq", 0, 0, tiled=True)
    before = shifted(near, 1)
    after = shifted(near, -1)
    diag_weights, diag_sum, diag_stats = diag_forward(queries, keys, values)
    everyone, diag_sum = lax.optimization_barrier((everyone, diag_sum))
    top_mine = everyone[:, 2 * OWN :]
    top_other = grp_swap(top_mine, 1)
    out_t, scaled, delta, kcat, sgrad, back, dmine, dother, dbefore, dafter = wide_attend(
        live, queries, out_grad, before, after, diag_sum, diag_stats,
        everyone, top_mine, top_other,
    )
    dmine = (dmine.astype(F32) + grp_swap(dother, 1).astype(F32)).astype(BF16)
    back = lax.dynamic_update_slice(back, dmine, (0, 2 * OWN, 0))
    back = lax.all_to_all(back, "seq", 0, 0, tiled=True)
    from_next = shifted(dbefore, -1)
    from_prev = shifted(dafter, 1)
    out, dq, diag = diag_backward(
        queries, keys, values, diag_weights, out_t, scaled, delta, kcat, sgrad
    )
    back, diag = lax.optimization_barrier((back, diag))
    group_up, top_up = collect(back)
    swapped = grp_swap(top_up, 2)
    dk, dv = finish(
        diag, near_pooled, from_prev, from_next, pooled, group_up, top_up, swapped
    )
    return out, dq, dk, dv


def solution(mesh):
    spec = P(("grp", "seq"), None)
    return jax.shard_map(
        per_device, mesh=mesh, in_specs=(spec,) * 4, out_specs=(spec,) * 4, check_vma=False
    )
```

```python
import math

import jax
import jax.numpy as jnp
from jax import lax
from jax.experimental import pallas as pl
from jax.experimental.pallas import tpu as pltpu
from jax.sharding import PartitionSpec as P

D = 1024
H = 16
HD = 64
PAIR = 2 * HD
PAIRS = D // PAIR
BLOCK = 512
BOTH = 2 * BLOCK
P1 = 4
P2 = 32
RATIO = 8
NEAR = BLOCK // P1
OWN = BLOCK // P2
N_SEQ = 32
GROUP = OWN * N_SEQ
TOP = 256
SENT = 2 * OWN + 8
WIDE = GROUP + TOP + 2 * NEAR
CHUNK = 256
ROWS = 128
TILES = BLOCK // ROWS
UNROLL = 2
LAG = 8
SOFT = 1.0 / math.sqrt(HD)

EPS = 1e-06
NEG = -1e30
LOG2E = math.log2(math.e)

F32 = jnp.float32
BF16 = jnp.bfloat16


def dot(a, b):
    return jnp.dot(a, b, preferred_element_type=F32)


def dot_rows(a, b):
    return lax.dot_general(a, b, (((1,), (1,)), ((), ())), preferred_element_type=F32)


def pieces(x, count):
    parts = []
    for _ in range(count):
        low = x.astype(BF16)
        parts.append(low)
        x = x - low.astype(F32)
    return parts


def pool_matrix(rows, cols, factor):
    row = lax.broadcasted_iota(jnp.int32, (rows, cols), 0)
    col = lax.broadcasted_iota(jnp.int32, (rows, cols), 1)
    return jnp.where(col // factor == row, 1.0, 0.0).astype(BF16)


def spread_matrix(rows, cols, factor):
    row = lax.broadcasted_iota(jnp.int32, (rows, cols), 0)
    col = lax.broadcasted_iota(jnp.int32, (rows, cols), 1)
    return jnp.where(row // factor == col, 1.0, 0.0).astype(BF16)


def head_means(count_pieces, *xs):
    width = 256
    row = lax.broadcasted_iota(jnp.int32, (width, width), 0)
    col = lax.broadcasted_iota(jnp.int32, (width, width), 1)
    same = jnp.where(row // HD == col // HD, 1.0 / HD, 0.0).astype(BF16)
    stack = [x[:, start : start + width] for x in xs for start in range(0, D, width)]
    stack = jnp.concatenate(stack, axis=0)
    count = stack.shape[0]
    found = dot(jnp.concatenate(pieces(stack, count_pieces), axis=0), same)
    found = sum(found[at : at + count] for at in range(0, count_pieces * count, count))
    means, at = [], 0
    for x in xs:
        rows = x.shape[0]
        tiles = [found[at + t * rows : at + t * rows + rows] for t in range(D // width)]
        means.append(jnp.concatenate(tiles, axis=1))
        at += rows * (D // width)
    return means


def normalize(*pooled):
    means = head_means(3, *[x * x for x in pooled])
    return [x * lax.rsqrt(mean + EPS) for x, mean in zip(pooled, means)]


def normalize_back(pooled, upstream):
    means = head_means(2, *[x * x for x in pooled], *[x * up for x, up in zip(pooled, upstream)])
    back = []
    for x, up, mean, inner in zip(pooled, upstream, means, means[len(pooled) :]):
        scale = lax.rsqrt(mean + EPS)
        back.append(scale * (up - x * (scale * scale * inner)))
    return back


def top_pool(rows):
    return jnp.mean(rows.astype(F32).reshape(rows.shape[0] // RATIO, RATIO, rows.shape[1]), axis=1)


def group_kernel(k_ref, v_ref, payload_ref, top_ref, pooled_ref, groups):
    tile = pl.program_id(0)
    for index, ref in enumerate((k_ref, v_ref)):
        groups[index, tile] = dot(pool_matrix(8, ROWS, P2), ref[...]) * (1.0 / P2)

    @pl.when(tile == TILES - 1)
    def _():
        pooled = []
        for index in range(2):
            parts = [groups[index, t][: ROWS // P2] for t in range(TILES)]
            pooled.append(jnp.concatenate(parts, axis=0))
            pooled_ref[index] = pooled[index]
        low = [group.astype(BF16) for group in normalize(*pooled)]
        for index, group in enumerate(low):
            payload_ref[:, index * OWN : index * OWN + OWN] = jnp.broadcast_to(
                group[None], (N_SEQ, OWN, D)
            )
        for index, top in enumerate(normalize(*[top_pool(group) for group in low])):
            top_ref[index] = top.astype(BF16)


def near_kernel(k_ref, v_ref, near_ref, near_pooled_ref):
    pooled = []
    for index, ref in enumerate((k_ref, v_ref)):
        pooled.append(dot(pool_matrix(ROWS // P1, ROWS, P1), ref[...]) * (1.0 / P1))
        near_pooled_ref[index] = pooled[index]
    for index, near in enumerate(normalize(*pooled)):
        near_ref[index] = near.astype(BF16)


def collect_kernel(back_ref, up_ref, top_ref):
    up_ref[...] = jnp.sum(back_ref[:, : 2 * OWN].astype(F32), axis=0).reshape(2, OWN, D)
    top_ref[...] = jnp.sum(back_ref[:, 2 * OWN :].astype(F32), axis=0)


def finish_kernel(
    diag_ref, near_pooled_ref, prev_ref, next_ref, pooled_ref, up_ref, top_ref, swapped_ref,
    dk_ref, dv_ref, spread,
):
    tile = pl.program_id(0)

    @pl.when(tile == 0)
    def _():
        pooled = [pooled_ref[0], pooled_ref[1]]
        tops = [top_pool(group.astype(BF16)) for group in normalize(*pooled)]
        top_up = [
            top_ref[4 * index : 4 * index + 2] + swapped_ref[4 * index + 2 : 4 * index + 4]
            for index in range(2)
        ]
        ups = []
        for index, back in enumerate(normalize_back(tops, top_up)):
            back = jnp.broadcast_to(back[:, None, :] * (1.0 / RATIO), (OWN // RATIO, RATIO, D))
            ups.append(up_ref[index] + back.reshape(OWN, D))
        for index, back in enumerate(normalize_back(pooled, ups)):
            spread[index] = back * (1.0 / P2)

    count = ROWS // P1
    near_up = [prev_ref[index].astype(F32) + next_ref[index].astype(F32) for index in range(2)]
    over = spread_matrix(ROWS, count, P1)
    over = jnp.concatenate([over, over], axis=1)
    near_back = normalize_back([near_pooled_ref[0], near_pooled_ref[1]], near_up)
    for index, out_ref in enumerate((dk_ref, dv_ref)):
        both = jnp.concatenate(pieces(near_back[index] * (1.0 / P1), 2), axis=0)
        total = diag_ref[index] + dot(over, both)
        for place in range(ROWS // P2):
            cut = slice(place * P2, place * P2 + P2)
            row = spread[index, pl.ds(tile * (ROWS // P2) + place, 1)]
            out_ref[cut] = (total[cut] + row).astype(BF16)


def starts(count):
    return range(0, count, CHUNK)


def apart(x_t):
    zero = jnp.zeros((HD, BLOCK), x_t.dtype)
    first = jnp.concatenate([x_t[:HD], zero], axis=1)
    second = jnp.concatenate([zero, x_t[HD:]], axis=1)
    return jnp.concatenate([first, second], axis=0)


def together(x):
    return jnp.concatenate([x[:HD, :BLOCK], x[HD:PAIR, BLOCK:]], axis=0)


def by_head(row):
    return jnp.concatenate(
        [jnp.broadcast_to(row[:, :BLOCK], (HD, BLOCK)), jnp.broadcast_to(row[:, BLOCK:], (HD, BLOCK))],
        axis=0,
    )


def head_sums(x):
    return jnp.concatenate(
        [jnp.sum(x[:HD], axis=0, keepdims=True), jnp.sum(x[HD:], axis=0, keepdims=True)], axis=1
    )


def head_rows(x):
    lane = lax.broadcasted_iota(jnp.int32, x.shape, 1)
    zero = jnp.zeros((), BF16)
    return jnp.concatenate([jnp.where(lane < HD, x, zero), jnp.where(lane < HD, zero, x)], axis=0)


def score_step(start, q_rows, kcat, scores, bias, largest):
    part = dot_rows(kcat[start : start + CHUNK], q_rows)
    if start in bias:
        part = part + bias[start]
    scores[start : start + CHUNK] = part
    part = jnp.max(part.reshape(CHUNK // 8, 8, BOTH), axis=0)
    return part if largest is None else jnp.maximum(largest, part)


def weight_step(start, scores, weights, largest):
    part = (scores[start : start + CHUNK] - largest) * (LOG2E * SOFT)
    weights[start : start + CHUNK] = jnp.exp2(part).astype(BF16)


def value_step(v_t, weights):
    found = dot(jnp.concatenate([v_t, jnp.ones((16, v_t.shape[1]), BF16)], axis=0), weights[...])
    return found[PAIR : PAIR + 1], together(found)


def grads_and_delta(scaled, delta):
    row = lax.broadcasted_iota(jnp.int32, (16, BOTH), 0)
    extra = jnp.zeros((16, BOTH), F32)
    for place, piece in enumerate(pieces(-delta, 3)):
        extra = jnp.where(row == place, piece.astype(F32), extra)
    zero = jnp.zeros((PAIR - 16, BOTH), BF16)
    return jnp.concatenate([apart(scaled), extra.astype(BF16), zero], axis=0)


def grad_step(start, g_both, vones, weights, sgrad):
    cut = slice(start, start + CHUNK)
    part = dot(vones[cut], g_both)
    sgrad[cut] = (part * weights[cut].astype(F32)).astype(BF16)


def diag_kernel(q_ref, k_ref, v_ref, g_ref, weights_ref, sum_ref, stats_ref, g_t_ref, scores):
    g_t_ref[...] = g_ref[...].T
    q_rows = head_rows(q_ref[...])
    largest = None
    for start in starts(BLOCK):
        largest = score_step(start, q_rows, k_ref, scores, {}, largest)
    largest = jnp.max(largest, axis=0, keepdims=True)
    for start in starts(BLOCK):
        weight_step(start, scores, weights_ref.at[0], largest)
    total, summed = value_step(v_ref[...].T, weights_ref.at[0])
    stats_ref[0, 0:1] = largest
    stats_ref[0, 1:2] = total
    sum_ref[...] = summed


def low_rows(shape):
    return lax.broadcasted_iota(jnp.int32, shape, 1) < 4


def split_top(ref, lanes):
    both = ref[:, :, lanes].astype(F32).reshape(N_SEQ // 2, 2, 8, PAIR)
    first, second = both[:, 0], both[:, 1]
    low = low_rows(first.shape)
    k = jnp.where(low, first, pltpu.roll(second, 4, 1))
    v = jnp.where(low, pltpu.roll(first, 4, 1), second)
    return k.reshape(TOP // 2, PAIR).astype(BF16), v.reshape(TOP // 2, PAIR).astype(BF16)


def join_top(k, v):
    k = k.reshape(N_SEQ // 2, 8, PAIR)
    v = v.reshape(N_SEQ // 2, 8, PAIR)
    low = low_rows(k.shape)
    first = jnp.where(low, k, pltpu.roll(v, 4, 1))
    second = jnp.where(low, pltpu.roll(k, 4, 1), v)
    return jnp.stack([first, second], axis=1).reshape(N_SEQ, 8, PAIR).astype(BF16)


def wide_kernel(
    live_ref, q_ref, g_ref, before_ref, after_ref, sum_ref, stats_ref,
    group_ref, mine_ref, other_ref,
    out_ref, scaled_ref, delta_ref, kcat_ref, sgrad_ref,
    dgroup_ref, dmine_ref, dother_ref, dbefore_ref, dafter_ref,
    vones, scores, weights,
):
    near_row = lax.broadcasted_iota(jnp.int32, (CHUNK, 1), 0)
    bias = {GROUP + TOP: jnp.where(near_row < NEAR, live_ref[0], live_ref[1])}

    @pl.when(pl.program_id(0) == 0)
    def _():
        vones[:, :, PAIR:] = jnp.ones((UNROLL, WIDE, PAIR), BF16)

    running = []
    for p in range(UNROLL):
        lanes = slice(p * PAIR, p * PAIR + PAIR)
        running.append(wide_pair(
            bias, q_ref.at[:, lanes], g_ref.at[lanes],
            before_ref.at[:, :, lanes], after_ref.at[:, :, lanes],
            sum_ref.at[lanes], stats_ref.at[p], group_ref.at[:, :, lanes],
            split_top(mine_ref, lanes), split_top(other_ref, lanes),
            out_ref.at[lanes], scaled_ref.at[lanes], delta_ref.at[p],
            kcat_ref.at[p], sgrad_ref.at[p],
            dgroup_ref.at[:, :, lanes], dmine_ref.at[:, :, lanes], dother_ref.at[:, :, lanes],
            dbefore_ref.at[:, :, lanes], dafter_ref.at[:, :, lanes],
            vones.at[p], scores.at[p], weights.at[p],
        ))
    staggered(running, LAG)


def staggered(running, lag):
    tick, left = 0, list(enumerate(running))
    while left:
        for item in list(left):
            index, steps = item
            if tick >= index * lag and next(steps, None) is None:
                left.remove(item)
        tick += 1


def wide_pair(
    bias, q_ref, g_ref, before_ref, after_ref, sum_ref, stats_ref, group_ref, mine, other,
    out_ref, scaled_ref, delta_ref, kcat, sgrad,
    dgroup_ref, dmine_ref, dother_ref, dbefore_ref, dafter_ref,
    vones, scores, weights,
):
    kcat[0:GROUP] = group_ref[:, 0:OWN].reshape(GROUP, PAIR)
    vones[0:GROUP, :PAIR] = group_ref[:, OWN : 2 * OWN].reshape(GROUP, PAIR)
    for start, (k, v) in ((GROUP, mine), (GROUP + TOP // 2, other)):
        kcat[start : start + TOP // 2] = k
        vones[start : start + TOP // 2, :PAIR] = v
    for start, ref in ((GROUP + TOP, before_ref), (GROUP + TOP + NEAR, after_ref)):
        kcat[start : start + NEAR] = ref[0]
        vones[start : start + NEAR, :PAIR] = ref[1]
    q_rows = head_rows(q_ref[...])
    largest = None
    for start in starts(WIDE):
        largest = score_step(start, q_rows, kcat, scores, bias, largest)
        yield True
    largest = jnp.max(largest, axis=0, keepdims=True)
    for start in starts(WIDE):
        weight_step(start, scores, weights, largest)
        yield True
    total, summed = value_step(vones[:, :PAIR].T, weights)
    yield True
    local_largest, local_total = stats_ref[0:1], stats_ref[1:2]
    most = jnp.maximum(largest, local_largest)
    share = jnp.exp2((largest - most) * (LOG2E * SOFT))
    local_share = jnp.exp2((local_largest - most) * (LOG2E * SOFT))
    inverse = 1.0 / (share * total + local_share * local_total)
    share = by_head(share * inverse)
    local_share = by_head(local_share * inverse)
    attended = share * summed + local_share * sum_ref[...]
    out_ref[...] = attended.astype(BF16)
    grad = g_ref[...].astype(F32)
    local_scaled = (grad * local_share).astype(BF16)
    scaled_ref[...] = local_scaled
    delta_ref[0:1] = head_sums(local_scaled.astype(F32) * attended)
    scaled = (grad * share).astype(BF16)
    g_both = grads_and_delta(scaled, head_sums(scaled.astype(F32) * attended))
    yield True
    for start in starts(WIDE):
        grad_step(start, g_both, vones, weights, sgrad)
        yield True
    g_rows = head_rows(scaled.T)
    for start in starts(WIDE):
        cut = slice(start, start + CHUNK)
        dk = dot(sgrad[cut], q_rows) * SOFT
        dv = dot(weights[cut], g_rows)
        if start < GROUP:
            devices = slice(start // OWN, (start + CHUNK) // OWN)
            shape = (CHUNK // OWN, OWN, PAIR)
            dgroup_ref[devices, 0:OWN] = dk.astype(BF16).reshape(shape)
            dgroup_ref[devices, OWN : 2 * OWN] = dv.astype(BF16).reshape(shape)
        elif start < GROUP + TOP:
            half = TOP // 2
            dmine_ref[...] = join_top(dk[:half], dv[:half])
            dother_ref[...] = join_top(dk[half:], dv[half:])
        else:
            for index, value in enumerate((dk, dv)):
                dbefore_ref[index] = value[:NEAR].astype(BF16)
                dafter_ref[index] = value[NEAR:].astype(BF16)
        yield True


def diag_back_kernel(
    q_ref, k_ref, v_ref, weights_ref, out_t_ref, scaled_ref, delta_ref, kcat_ref, wide_ref,
    out_ref, dq_ref, diag_ref, vones, sgrad,
):
    @pl.when(pl.program_id(0) == 0)
    def _():
        vones[:, PAIR:] = jnp.ones((BLOCK, PAIR), BF16)

    vones[:, :PAIR] = v_ref[...]
    out_ref[...] = out_t_ref[...].T
    weights = weights_ref.at[0]
    scaled = scaled_ref[...]
    g_both = grads_and_delta(scaled, delta_ref[0, 0:1])
    for start in starts(BLOCK):
        grad_step(start, g_both, vones, weights, sgrad)
    dq = dot(kcat_ref[0].T, wide_ref[0]) + dot(k_ref[...].T, sgrad[...])
    dq_ref[...] = (together(dq).T * SOFT).astype(BF16)
    q_rows = head_rows(q_ref[...])
    g_rows = head_rows(scaled.T)
    for start in starts(BLOCK):
        cut = slice(start, start + CHUNK)
        diag_ref[0, cut] = dot(sgrad[cut], q_rows) * SOFT
        diag_ref[1, cut] = dot(weights[cut], g_rows)


def shape_of(dtype, *shape):
    return jax.ShapeDtypeStruct(shape, dtype)


def on_lanes(*lead):
    return pl.BlockSpec(lead + (PAIR,), lambda p: (0,) * len(lead) + (p,))


def on_rows(*shape):
    return pl.BlockSpec(shape, lambda p: (p,) + (0,) * (len(shape) - 1))


def on_middle(*shape):
    return pl.BlockSpec(shape, lambda p: (0, p, 0))


def every(*shape):
    return pl.BlockSpec(shape, lambda p: (0,) * len(shape))


SMEM = pl.BlockSpec(memory_space=pltpu.SMEM)
SEQUENCE = on_lanes(BLOCK)
COLUMNS = on_rows(PAIR, BLOCK)
STATS = on_rows(1, 8, BOTH)
DIAG = on_rows(1, BLOCK, BOTH)
WIDE_KEYS = on_rows(1, WIDE, PAIR)
WIDE_GRADS = on_rows(1, WIDE, BOTH)


def call(kernel, name, steps, in_specs, out_specs, out_shape, scratch=()):
    return pl.pallas_call(
        kernel,
        grid=(steps,),
        in_specs=in_specs,
        out_specs=out_specs,
        out_shape=out_shape,
        scratch_shapes=scratch,
        compiler_params=pltpu.CompilerParams(vmem_limit_bytes=56 * 1024 * 1024),
        name=name,
    )


group_summaries = call(
    group_kernel,
    "group_summaries",
    TILES,
    [on_rows(ROWS, D)] * 2,
    [every(N_SEQ, 2 * OWN, D), every(2, OWN // RATIO, D), every(2, OWN, D)],
    (
        shape_of(BF16, N_SEQ, SENT, D),
        shape_of(BF16, 2, OWN // RATIO, D),
        shape_of(F32, 2, OWN, D),
    ),
    [pltpu.VMEM((2, TILES, 8, D), F32)],
)
near_summaries = call(
    near_kernel,
    "near_summaries",
    TILES,
    [on_rows(ROWS, D)] * 2,
    [on_middle(2, ROWS // P1, D)] * 2,
    (shape_of(BF16, 2, NEAR, D), shape_of(F32, 2, NEAR, D)),
)
diag_forward = call(
    diag_kernel,
    "diag_forward",
    PAIRS,
    [SEQUENCE] * 4,
    [DIAG, COLUMNS, STATS, COLUMNS],
    (
        shape_of(BF16, PAIRS, BLOCK, BOTH),
        shape_of(F32, D, BLOCK),
        shape_of(F32, PAIRS, 8, BOTH),
        shape_of(BF16, D, BLOCK),
    ),
    [pltpu.VMEM((BLOCK, BOTH), F32)],
)
def wide_lanes(*lead):
    return pl.BlockSpec(lead + (UNROLL * PAIR,), lambda p: (0,) * len(lead) + (p,))


wide_attend = call(
    wide_kernel,
    "wide_attend",
    PAIRS // UNROLL,
    [SMEM]
    + [wide_lanes(BLOCK), on_rows(UNROLL * PAIR, BLOCK)]
    + [wide_lanes(2, NEAR)] * 2
    + [on_rows(UNROLL * PAIR, BLOCK), on_rows(UNROLL, 8, BOTH)]
    + [wide_lanes(N_SEQ, 2 * OWN)]
    + [wide_lanes(N_SEQ, 8)] * 2,
    [on_rows(UNROLL * PAIR, BLOCK)] * 2
    + [on_rows(UNROLL, 8, BOTH), on_rows(UNROLL, WIDE, PAIR), on_rows(UNROLL, WIDE, BOTH)]
    + [wide_lanes(N_SEQ, 2 * OWN)]
    + [wide_lanes(N_SEQ, 8)] * 2
    + [wide_lanes(2, NEAR)] * 2,
    (
        shape_of(BF16, D, BLOCK),
        shape_of(BF16, D, BLOCK),
        shape_of(F32, PAIRS, 8, BOTH),
        shape_of(BF16, PAIRS, WIDE, PAIR),
        shape_of(BF16, PAIRS, WIDE, BOTH),
        shape_of(BF16, N_SEQ, SENT, D),
        shape_of(BF16, N_SEQ, 8, D),
        shape_of(BF16, N_SEQ, 8, D),
    )
    + (shape_of(BF16, 2, NEAR, D),) * 2,
    [
        pltpu.VMEM((UNROLL, WIDE, 2 * PAIR), BF16),
        pltpu.VMEM((UNROLL, WIDE, BOTH), F32),
        pltpu.VMEM((UNROLL, WIDE, BOTH), BF16),
    ],
)
diag_backward = call(
    diag_back_kernel,
    "diag_backward",
    PAIRS,
    [SEQUENCE] * 3 + [DIAG] + [COLUMNS] * 2 + [STATS, WIDE_KEYS, WIDE_GRADS],
    [SEQUENCE, SEQUENCE, on_lanes(2, BLOCK)],
    (shape_of(BF16, BLOCK, D), shape_of(BF16, BLOCK, D), shape_of(F32, 2, BLOCK, D)),
    [pltpu.VMEM((BLOCK, 2 * PAIR), BF16), pltpu.VMEM((BLOCK, BOTH), BF16)],
)
collect = pl.pallas_call(
    collect_kernel,
    out_shape=(shape_of(F32, 2, OWN, D), shape_of(F32, 8, D)),
    compiler_params=pltpu.CompilerParams(vmem_limit_bytes=16 * 1024 * 1024),
    name="collect",
)
finish = call(
    finish_kernel,
    "finish",
    TILES,
    [on_middle(2, ROWS, D)]
    + [on_middle(2, ROWS // P1, D)] * 3
    + [every(2, OWN, D)] * 2
    + [every(8, D)] * 2,
    [on_rows(ROWS, D)] * 2,
    (shape_of(BF16, BLOCK, D), shape_of(BF16, BLOCK, D)),
    [pltpu.VMEM((2, OWN, D), F32)],
)


def shifted(block, distance):
    count = lax.axis_size(("grp", "seq"))
    route = [(i, i + distance) for i in range(count) if 0 <= i + distance < count]
    return lax.ppermute(block, ("grp", "seq"), route)


def grp_swap(block, bit):
    return lax.ppermute(block, "grp", [(i, i ^ bit) for i in range(4)])


def per_device(queries, keys, values, out_grad):
    device = lax.axis_index("grp") * N_SEQ + lax.axis_index("seq")
    count = lax.axis_size(("grp", "seq"))
    live = jnp.stack(
        [jnp.where(device == 0, NEG, 0.0), jnp.where(device == count - 1, NEG, 0.0)]
    ).astype(F32)
    payload, top, pooled = group_summaries(keys, values)
    swapped = grp_swap(top, 2)
    near, near_pooled = near_summaries(keys, values)
    near, live = lax.optimization_barrier((near, live))
    top_pair = jnp.stack([top, swapped], axis=1).reshape(8, D)
    tops = jnp.broadcast_to(top_pair[None], (N_SEQ, 8, D))
    payload = lax.dynamic_update_slice(payload, tops, (0, 2 * OWN, 0))
    everyone = lax.all_to_all(payload, "seq", 0, 0, tiled=True)
    before = shifted(near, 1)
    after = shifted(near, -1)
    diag_weights, diag_sum, diag_stats, grad_t = diag_forward(queries, keys, values, out_grad)
    everyone, diag_sum = lax.optimization_barrier((everyone, diag_sum))
    top_mine = everyone[:, 2 * OWN :]
    top_other = grp_swap(top_mine, 1)
    out_t, scaled, delta, kcat, sgrad, back, dmine, dother, dbefore, dafter = wide_attend(
        live, queries, grad_t, before, after, diag_sum, diag_stats,
        everyone, top_mine, top_other,
    )
    dmine = (dmine.astype(F32) + grp_swap(dother, 1).astype(F32)).astype(BF16)
    back = lax.dynamic_update_slice(back, dmine, (0, 2 * OWN, 0))
    back = lax.all_to_all(back, "seq", 0, 0, tiled=True)
    from_next = shifted(dbefore, -1)
    from_prev = shifted(dafter, 1)
    out, dq, diag = diag_backward(
        queries, keys, values, diag_weights, out_t, scaled, delta, kcat, sgrad
    )
    back, diag = lax.optimization_barrier((back, diag))
    group_up, top_up = collect(back)
    swapped = grp_swap(top_up, 2)
    dk, dv = finish(
        diag, near_pooled, from_prev, from_next, pooled, group_up, top_up, swapped
    )
    return out, dq, dk, dv


def solution(mesh):
    spec = P(("grp", "seq"), None)
    return jax.shard_map(
        per_device, mesh=mesh, in_specs=(spec,) * 4, out_specs=(spec,) * 4, check_vma=False
    )
```

```python
import functools
import math

import jax
import jax.numpy as jnp
from jax import lax
from jax.experimental import pallas as pl
from jax.experimental.pallas import tpu as pltpu
from jax.sharding import PartitionSpec as P

D = 1024
H = 16
HD = 64
PAIR = 2 * HD
PAIRS = D // PAIR
BLOCK = 512
BOTH = 2 * BLOCK
P1 = 4
P2 = 32
RATIO = 8
NEAR = BLOCK // P1
OWN = BLOCK // P2
N_SEQ = 32
GROUP = OWN * N_SEQ
TOP = 256
SENT = 2 * OWN + 8
WIDE = GROUP + TOP + 2 * NEAR
CHUNK = 256
ROWS = 128
TILES = BLOCK // ROWS
UNROLL = 2
PARTS = 2
LANES = D // PARTS
PART_STEPS = PAIRS // PARTS // UNROLL
LAG = 8
SOFT = 1.0 / math.sqrt(HD)

EPS = 1e-06
NEG = -1e30
LOG2E = math.log2(math.e)

F32 = jnp.float32
BF16 = jnp.bfloat16


def dot(a, b):
    return jnp.dot(a, b, preferred_element_type=F32)


def dot_rows(a, b):
    return lax.dot_general(a, b, (((1,), (1,)), ((), ())), preferred_element_type=F32)


def pieces(x, count):
    parts = []
    for _ in range(count):
        low = x.astype(BF16)
        parts.append(low)
        x = x - low.astype(F32)
    return parts


def pool_matrix(rows, cols, factor):
    row = lax.broadcasted_iota(jnp.int32, (rows, cols), 0)
    col = lax.broadcasted_iota(jnp.int32, (rows, cols), 1)
    return jnp.where(col // factor == row, 1.0, 0.0).astype(BF16)


def spread_matrix(rows, cols, factor):
    row = lax.broadcasted_iota(jnp.int32, (rows, cols), 0)
    col = lax.broadcasted_iota(jnp.int32, (rows, cols), 1)
    return jnp.where(row // factor == col, 1.0, 0.0).astype(BF16)


def head_means(count_pieces, *xs):
    width = 256
    row = lax.broadcasted_iota(jnp.int32, (width, width), 0)
    col = lax.broadcasted_iota(jnp.int32, (width, width), 1)
    same = jnp.where(row // HD == col // HD, 1.0 / HD, 0.0).astype(BF16)
    stack = [x[:, start : start + width] for x in xs for start in range(0, D, width)]
    stack = jnp.concatenate(stack, axis=0)
    count = stack.shape[0]
    found = dot(jnp.concatenate(pieces(stack, count_pieces), axis=0), same)
    found = sum(found[at : at + count] for at in range(0, count_pieces * count, count))
    means, at = [], 0
    for x in xs:
        rows = x.shape[0]
        tiles = [found[at + t * rows : at + t * rows + rows] for t in range(D // width)]
        means.append(jnp.concatenate(tiles, axis=1))
        at += rows * (D // width)
    return means


def normalize(*pooled):
    means = head_means(3, *[x * x for x in pooled])
    return [x * lax.rsqrt(mean + EPS) for x, mean in zip(pooled, means)]


def normalize_back(pooled, upstream):
    means = head_means(2, *[x * x for x in pooled], *[x * up for x, up in zip(pooled, upstream)])
    back = []
    for x, up, mean, inner in zip(pooled, upstream, means, means[len(pooled) :]):
        scale = lax.rsqrt(mean + EPS)
        back.append(scale * (up - x * (scale * scale * inner)))
    return back


def top_pool(rows):
    return jnp.mean(rows.astype(F32).reshape(rows.shape[0] // RATIO, RATIO, rows.shape[1]), axis=1)


def group_kernel(k_ref, v_ref, top_ref, pooled_ref, *rest):
    payloads, groups = rest[:PARTS], rest[PARTS]
    tile = pl.program_id(0)
    for index, ref in enumerate((k_ref, v_ref)):
        groups[index, tile] = dot(pool_matrix(8, ROWS, P2), ref[...]) * (1.0 / P2)

    @pl.when(tile == TILES - 1)
    def _():
        pooled = []
        for index in range(2):
            parts = [groups[index, t][: ROWS // P2] for t in range(TILES)]
            pooled.append(jnp.concatenate(parts, axis=0))
            pooled_ref[index] = pooled[index]
        low = [group.astype(BF16) for group in normalize(*pooled)]
        for index, group in enumerate(low):
            for part, payload_ref in enumerate(payloads):
                lanes = slice(part * LANES, part * LANES + LANES)
                payload_ref[:, index * OWN : index * OWN + OWN] = jnp.broadcast_to(
                    group[None, :, lanes], (N_SEQ, OWN, LANES)
                )
        for index, top in enumerate(normalize(*[top_pool(group) for group in low])):
            top_ref[index] = top.astype(BF16)


def near_kernel(k_ref, v_ref, near_ref, near_pooled_ref):
    pooled = []
    for index, ref in enumerate((k_ref, v_ref)):
        pooled.append(dot(pool_matrix(ROWS // P1, ROWS, P1), ref[...]) * (1.0 / P1))
        near_pooled_ref[index] = pooled[index]
    for index, near in enumerate(normalize(*pooled)):
        near_ref[index] = near.astype(BF16)


def collect_kernel(*refs):
    backs, (up_ref, top_ref) = refs[:PARTS], refs[PARTS:]
    for part, back_ref in enumerate(backs):
        lanes = slice(part * LANES, part * LANES + LANES)
        total = jnp.sum(back_ref[:, : 2 * OWN].astype(F32), axis=0)
        up_ref[:, :, lanes] = total.reshape(2, OWN, LANES)
        top_ref[:, lanes] = jnp.sum(back_ref[:, 2 * OWN :].astype(F32), axis=0)


def finish_kernel(
    diag_ref, near_pooled_ref, prev_ref, next_ref, pooled_ref, up_ref, top_ref, swapped_ref,
    dk_ref, dv_ref, spread,
):
    tile = pl.program_id(0)

    @pl.when(tile == 0)
    def _():
        pooled = [pooled_ref[0], pooled_ref[1]]
        tops = [top_pool(group.astype(BF16)) for group in normalize(*pooled)]
        top_up = [
            top_ref[4 * index : 4 * index + 2] + swapped_ref[4 * index + 2 : 4 * index + 4]
            for index in range(2)
        ]
        ups = []
        for index, back in enumerate(normalize_back(tops, top_up)):
            back = jnp.broadcast_to(back[:, None, :] * (1.0 / RATIO), (OWN // RATIO, RATIO, D))
            ups.append(up_ref[index] + back.reshape(OWN, D))
        for index, back in enumerate(normalize_back(pooled, ups)):
            spread[index] = back * (1.0 / P2)

    count = ROWS // P1
    near_up = [prev_ref[index].astype(F32) + next_ref[index].astype(F32) for index in range(2)]
    over = spread_matrix(ROWS, count, P1)
    over = jnp.concatenate([over, over], axis=1)
    near_back = normalize_back([near_pooled_ref[0], near_pooled_ref[1]], near_up)
    for index, out_ref in enumerate((dk_ref, dv_ref)):
        both = jnp.concatenate(pieces(near_back[index] * (1.0 / P1), 2), axis=0)
        total = diag_ref[index] + dot(over, both)
        for place in range(ROWS // P2):
            cut = slice(place * P2, place * P2 + P2)
            row = spread[index, pl.ds(tile * (ROWS // P2) + place, 1)]
            out_ref[cut] = (total[cut] + row).astype(BF16)


def starts(count):
    return range(0, count, CHUNK)


def apart(x_t):
    zero = jnp.zeros((HD, BLOCK), x_t.dtype)
    first = jnp.concatenate([x_t[:HD], zero], axis=1)
    second = jnp.concatenate([zero, x_t[HD:]], axis=1)
    return jnp.concatenate([first, second], axis=0)


def together(x):
    return jnp.concatenate([x[:HD, :BLOCK], x[HD:PAIR, BLOCK:]], axis=0)


def by_head(row):
    return jnp.concatenate(
        [jnp.broadcast_to(row[:, :BLOCK], (HD, BLOCK)), jnp.broadcast_to(row[:, BLOCK:], (HD, BLOCK))],
        axis=0,
    )


def head_sums(x):
    return jnp.concatenate(
        [jnp.sum(x[:HD], axis=0, keepdims=True), jnp.sum(x[HD:], axis=0, keepdims=True)], axis=1
    )


def head_rows(x):
    lane = lax.broadcasted_iota(jnp.int32, x.shape, 1)
    zero = jnp.zeros((), BF16)
    return jnp.concatenate([jnp.where(lane < HD, x, zero), jnp.where(lane < HD, zero, x)], axis=0)


def score_step(start, q_rows, kcat, scores, bias, largest):
    part = dot_rows(kcat[start : start + CHUNK], q_rows)
    if start in bias:
        part = part + bias[start]
    scores[start : start + CHUNK] = part
    part = jnp.max(part.reshape(CHUNK // 8, 8, BOTH), axis=0)
    return part if largest is None else jnp.maximum(largest, part)


def weight_step(start, scores, weights, largest):
    part = (scores[start : start + CHUNK] - largest) * (LOG2E * SOFT)
    weights[start : start + CHUNK] = jnp.exp2(part).astype(BF16)


def value_step(v_t, weights):
    found = dot(jnp.concatenate([v_t, jnp.ones((16, v_t.shape[1]), BF16)], axis=0), weights[...])
    return found[PAIR : PAIR + 1], together(found)


def grads_and_delta(scaled, delta):
    row = lax.broadcasted_iota(jnp.int32, (16, BOTH), 0)
    extra = jnp.zeros((16, BOTH), F32)
    for place, piece in enumerate(pieces(-delta, 3)):
        extra = jnp.where(row == place, piece.astype(F32), extra)
    zero = jnp.zeros((PAIR - 16, BOTH), BF16)
    return jnp.concatenate([apart(scaled), extra.astype(BF16), zero], axis=0)


def grad_step(start, g_both, vones, weights, sgrad):
    cut = slice(start, start + CHUNK)
    part = dot(vones[cut], g_both)
    sgrad[cut] = (part * weights[cut].astype(F32)).astype(BF16)


def pair_lanes():
    return [(p, slice(p * PAIR, p * PAIR + PAIR)) for p in range(UNROLL)]


def diag_kernel(q_ref, k_ref, v_ref, g_ref, weights_ref, sum_ref, stats_ref, g_t_ref, scores):
    running = [
        diag_pair(
            q_ref.at[:, lanes], k_ref.at[:, lanes], v_ref.at[:, lanes], g_ref.at[:, lanes],
            weights_ref.at[p], sum_ref.at[lanes], stats_ref.at[p], g_t_ref.at[lanes], scores.at[p],
        )
        for p, lanes in pair_lanes()
    ]
    staggered(running, BLOCK // CHUNK)


def diag_pair(q_ref, k_ref, v_ref, g_ref, weights, sum_ref, stats_ref, g_t_ref, scores):
    g_t_ref[...] = g_ref[...].T
    q_rows = head_rows(q_ref[...])
    largest = None
    for start in starts(BLOCK):
        largest = score_step(start, q_rows, k_ref, scores, {}, largest)
        yield True
    largest = jnp.max(largest, axis=0, keepdims=True)
    for start in starts(BLOCK):
        weight_step(start, scores, weights, largest)
        yield True
    total, summed = value_step(v_ref[...].T, weights)
    stats_ref[0:1] = largest
    stats_ref[1:2] = total
    sum_ref[...] = summed
    yield True


def low_rows(shape):
    return lax.broadcasted_iota(jnp.int32, shape, 1) < 4


def split_top(ref, lanes):
    both = ref[:, :, lanes].astype(F32).reshape(N_SEQ // 2, 2, 8, PAIR)
    first, second = both[:, 0], both[:, 1]
    low = low_rows(first.shape)
    k = jnp.where(low, first, pltpu.roll(second, 4, 1))
    v = jnp.where(low, pltpu.roll(first, 4, 1), second)
    return k.reshape(TOP // 2, PAIR).astype(BF16), v.reshape(TOP // 2, PAIR).astype(BF16)


def join_top(k, v):
    k = k.reshape(N_SEQ // 2, 8, PAIR)
    v = v.reshape(N_SEQ // 2, 8, PAIR)
    low = low_rows(k.shape)
    first = jnp.where(low, k, pltpu.roll(v, 4, 1))
    second = jnp.where(low, pltpu.roll(k, 4, 1), v)
    return jnp.stack([first, second], axis=1).reshape(N_SEQ, 8, PAIR).astype(BF16)


def wide_kernel(
    live_ref, q_ref, g_ref, before_ref, after_ref, sum_ref, stats_ref,
    group_ref, mine_ref, other_ref, *rest,
):
    (
        out_ref, scaled_ref, delta_ref, kcat_ref, sgrad_ref, dbefore_ref, dafter_ref,
        dgroup_ref, dmine_ref, dother_ref, vones, scores, weights,
    ) = rest[-13:]
    near_row = lax.broadcasted_iota(jnp.int32, (CHUNK, 1), 0)
    bias = {GROUP + TOP: jnp.where(near_row < NEAR, live_ref[0], live_ref[1])}

    @pl.when(pl.program_id(0) == 0)
    def _():
        vones[:, :, PAIR:] = jnp.ones((UNROLL, WIDE, PAIR), BF16)

    running = []
    for p in range(UNROLL):
        lanes = slice(p * PAIR, p * PAIR + PAIR)
        running.append(wide_pair(
            bias, q_ref.at[:, lanes], g_ref.at[lanes],
            before_ref.at[:, :, lanes], after_ref.at[:, :, lanes],
            sum_ref.at[lanes], stats_ref.at[p], group_ref.at[:, :, lanes],
            split_top(mine_ref, lanes), split_top(other_ref, lanes),
            out_ref.at[lanes], scaled_ref.at[lanes], delta_ref.at[p],
            kcat_ref.at[p], sgrad_ref.at[p],
            dgroup_ref.at[:, :, lanes], dmine_ref.at[:, :, lanes], dother_ref.at[:, :, lanes],
            dbefore_ref.at[:, :, lanes], dafter_ref.at[:, :, lanes],
            vones.at[p], scores.at[p], weights.at[p],
        ))
    staggered(running, LAG)


def staggered(running, lag):
    tick, left = 0, list(enumerate(running))
    while left:
        for item in list(left):
            index, steps = item
            if tick >= index * lag and next(steps, None) is None:
                left.remove(item)
        tick += 1


def wide_pair(
    bias, q_ref, g_ref, before_ref, after_ref, sum_ref, stats_ref, group_ref, mine, other,
    out_ref, scaled_ref, delta_ref, kcat, sgrad,
    dgroup_ref, dmine_ref, dother_ref, dbefore_ref, dafter_ref,
    vones, scores, weights,
):
    kcat[0:GROUP] = group_ref[:, 0:OWN].reshape(GROUP, PAIR)
    vones[0:GROUP, :PAIR] = group_ref[:, OWN : 2 * OWN].reshape(GROUP, PAIR)
    for start, (k, v) in ((GROUP, mine), (GROUP + TOP // 2, other)):
        kcat[start : start + TOP // 2] = k
        vones[start : start + TOP // 2, :PAIR] = v
    for start, ref in ((GROUP + TOP, before_ref), (GROUP + TOP + NEAR, after_ref)):
        kcat[start : start + NEAR] = ref[0]
        vones[start : start + NEAR, :PAIR] = ref[1]
    q_rows = head_rows(q_ref[...])
    largest = None
    for start in starts(WIDE):
        largest = score_step(start, q_rows, kcat, scores, bias, largest)
        yield True
    largest = jnp.max(largest, axis=0, keepdims=True)
    for start in starts(WIDE):
        weight_step(start, scores, weights, largest)
        yield True
    total, summed = value_step(vones[:, :PAIR].T, weights)
    yield True
    local_largest, local_total = stats_ref[0:1], stats_ref[1:2]
    most = jnp.maximum(largest, local_largest)
    share = jnp.exp2((largest - most) * (LOG2E * SOFT))
    local_share = jnp.exp2((local_largest - most) * (LOG2E * SOFT))
    inverse = 1.0 / (share * total + local_share * local_total)
    share = by_head(share * inverse)
    local_share = by_head(local_share * inverse)
    attended = share * summed + local_share * sum_ref[...]
    out_ref[...] = attended.astype(BF16)
    grad = g_ref[...].astype(F32)
    local_scaled = (grad * local_share).astype(BF16)
    scaled_ref[...] = local_scaled
    delta_ref[0:1] = head_sums(local_scaled.astype(F32) * attended)
    scaled = (grad * share).astype(BF16)
    g_both = grads_and_delta(scaled, head_sums(scaled.astype(F32) * attended))
    yield True
    for start in starts(WIDE):
        grad_step(start, g_both, vones, weights, sgrad)
        yield True
    g_rows = head_rows(scaled.T)
    for start in starts(WIDE):
        cut = slice(start, start + CHUNK)
        dk = dot(sgrad[cut], q_rows) * SOFT
        dv = dot(weights[cut], g_rows)
        if start < GROUP:
            devices = slice(start // OWN, (start + CHUNK) // OWN)
            shape = (CHUNK // OWN, OWN, PAIR)
            dgroup_ref[devices, 0:OWN] = dk.astype(BF16).reshape(shape)
            dgroup_ref[devices, OWN : 2 * OWN] = dv.astype(BF16).reshape(shape)
        elif start < GROUP + TOP:
            half = TOP // 2
            dmine_ref[...] = join_top(dk[:half], dv[:half])
            dother_ref[...] = join_top(dk[half:], dv[half:])
        else:
            for index, value in enumerate((dk, dv)):
                dbefore_ref[index] = value[:NEAR].astype(BF16)
                dafter_ref[index] = value[NEAR:].astype(BF16)
        yield True


def diag_back_kernel(
    q_ref, k_ref, v_ref, weights_ref, out_t_ref, scaled_ref, delta_ref, kcat_ref, wide_ref,
    out_ref, dq_ref, diag_ref, vones, sgrad,
):
    @pl.when(pl.program_id(0) == 0)
    def _():
        vones[:, :, PAIR:] = jnp.ones((UNROLL, BLOCK, PAIR), BF16)

    running = [
        diag_back_pair(
            q_ref.at[:, lanes], k_ref.at[:, lanes], v_ref.at[:, lanes], weights_ref.at[p],
            out_t_ref.at[lanes], scaled_ref.at[lanes], delta_ref.at[p], kcat_ref.at[p],
            wide_ref.at[p], out_ref.at[:, lanes], dq_ref.at[:, lanes], diag_ref.at[:, :, lanes],
            vones.at[p], sgrad.at[p],
        )
        for p, lanes in pair_lanes()
    ]
    staggered(running, BLOCK // CHUNK)


def diag_back_pair(
    q_ref, k_ref, v_ref, weights, out_t_ref, scaled_ref, delta_ref, kcat, wide,
    out_ref, dq_ref, diag_ref, vones, sgrad,
):
    vones[:, :PAIR] = v_ref[...]
    out_ref[...] = out_t_ref[...].T
    scaled = scaled_ref[...]
    g_both = grads_and_delta(scaled, delta_ref[0:1])
    for start in starts(BLOCK):
        grad_step(start, g_both, vones, weights, sgrad)
        yield True
    dq = dot(kcat[...].T, wide[...]) + dot(k_ref[...].T, sgrad[...])
    dq_ref[...] = (together(dq).T * SOFT).astype(BF16)
    yield True
    q_rows = head_rows(q_ref[...])
    g_rows = head_rows(scaled.T)
    for start in starts(BLOCK):
        cut = slice(start, start + CHUNK)
        diag_ref[0, cut] = dot(sgrad[cut], q_rows) * SOFT
        diag_ref[1, cut] = dot(weights[cut], g_rows)
        yield True


def shape_of(dtype, *shape):
    return jax.ShapeDtypeStruct(shape, dtype)


def on_lanes(*lead):
    return pl.BlockSpec(lead + (UNROLL * PAIR,), lambda p: (0,) * len(lead) + (p,))


def on_rows(*shape):
    return pl.BlockSpec(shape, lambda p: (p,) + (0,) * (len(shape) - 1))


def on_middle(*shape):
    return pl.BlockSpec(shape, lambda p: (0, p, 0))


def every(*shape):
    return pl.BlockSpec(shape, lambda p: (0,) * len(shape))


SMEM = pl.BlockSpec(memory_space=pltpu.SMEM)
SEQUENCE = on_lanes(BLOCK)
COLUMNS = on_rows(UNROLL * PAIR, BLOCK)
STATS = on_rows(UNROLL, 8, BOTH)
DIAG = on_rows(UNROLL, BLOCK, BOTH)
WIDE_KEYS = on_rows(UNROLL, WIDE, PAIR)
WIDE_GRADS = on_rows(UNROLL, WIDE, BOTH)


def call(kernel, name, steps, in_specs, out_specs, out_shape, scratch=()):
    return pl.pallas_call(
        kernel,
        grid=(steps,),
        in_specs=in_specs,
        out_specs=out_specs,
        out_shape=out_shape,
        scratch_shapes=scratch,
        compiler_params=pltpu.CompilerParams(vmem_limit_bytes=56 * 1024 * 1024),
        name=name,
    )


group_summaries = call(
    group_kernel,
    "group_summaries",
    TILES,
    [on_rows(ROWS, D)] * 2,
    [every(2, OWN // RATIO, D), every(2, OWN, D)] + [every(N_SEQ, 2 * OWN, LANES)] * PARTS,
    (shape_of(BF16, 2, OWN // RATIO, D), shape_of(F32, 2, OWN, D))
    + (shape_of(BF16, N_SEQ, SENT, LANES),) * PARTS,
    [pltpu.VMEM((2, TILES, 8, D), F32)],
)
near_summaries = call(
    near_kernel,
    "near_summaries",
    TILES,
    [on_rows(ROWS, D)] * 2,
    [on_middle(2, ROWS // P1, D)] * 2,
    (shape_of(BF16, 2, NEAR, D), shape_of(F32, 2, NEAR, D)),
)
diag_forward = call(
    diag_kernel,
    "diag_forward",
    PAIRS // UNROLL,
    [SEQUENCE] * 4,
    [DIAG, COLUMNS, STATS, COLUMNS],
    (
        shape_of(BF16, PAIRS, BLOCK, BOTH),
        shape_of(F32, D, BLOCK),
        shape_of(F32, PAIRS, 8, BOTH),
        shape_of(BF16, D, BLOCK),
    ),
    [pltpu.VMEM((UNROLL, BLOCK, BOTH), F32)],
)
def wide_attend(part, *args):
    offset = part * PART_STEPS

    def part_lanes(*lead):
        return pl.BlockSpec(lead + (UNROLL * PAIR,), lambda p: (0,) * len(lead) + (p,))

    def wide_lanes(*lead):
        return pl.BlockSpec(
            lead + (UNROLL * PAIR,), lambda p: (0,) * len(lead) + (p + offset,)
        )

    def wide_rows(*shape):
        return pl.BlockSpec(shape, lambda p: (p + offset,) + (0,) * (len(shape) - 1))

    in_specs = (
        [SMEM, wide_lanes(BLOCK), wide_rows(UNROLL * PAIR, BLOCK)]
        + [wide_lanes(2, NEAR)] * 2
        + [wide_rows(UNROLL * PAIR, BLOCK), wide_rows(UNROLL, 8, BOTH)]
        + [part_lanes(N_SEQ, 2 * OWN)]
        + [part_lanes(N_SEQ, 8)] * 2
    )
    shared = len(args) - len(in_specs)
    aliases = {len(in_specs) + index: index for index in range(shared)}
    return pl.pallas_call(
        wide_kernel,
        grid=(PART_STEPS,),
        in_specs=in_specs + [pl.BlockSpec(memory_space=pl.ANY)] * shared,
        out_specs=[wide_rows(UNROLL * PAIR, BLOCK)] * 2
        + [wide_rows(UNROLL, 8, BOTH), wide_rows(UNROLL, WIDE, PAIR)]
        + [wide_rows(UNROLL, WIDE, BOTH)]
        + [wide_lanes(2, NEAR)] * 2
        + [part_lanes(N_SEQ, 2 * OWN)]
        + [part_lanes(N_SEQ, 8)] * 2,
        out_shape=(
            shape_of(BF16, D, BLOCK),
            shape_of(BF16, D, BLOCK),
            shape_of(F32, PAIRS, 8, BOTH),
            shape_of(BF16, PAIRS, WIDE, PAIR),
            shape_of(BF16, PAIRS, WIDE, BOTH),
            shape_of(BF16, 2, NEAR, D),
            shape_of(BF16, 2, NEAR, D),
            shape_of(BF16, N_SEQ, SENT, LANES),
            shape_of(BF16, N_SEQ, 8, LANES),
            shape_of(BF16, N_SEQ, 8, LANES),
        ),
        scratch_shapes=[
            pltpu.VMEM((UNROLL, WIDE, 2 * PAIR), BF16),
            pltpu.VMEM((UNROLL, WIDE, BOTH), F32),
            pltpu.VMEM((UNROLL, WIDE, BOTH), BF16),
        ],
        input_output_aliases=aliases,
        compiler_params=pltpu.CompilerParams(vmem_limit_bytes=56 * 1024 * 1024),
        name="wide_attend%d" % part,
    )(*args)


diag_backward = call(
    diag_back_kernel,
    "diag_backward",
    PAIRS // UNROLL,
    [SEQUENCE] * 3 + [DIAG] + [COLUMNS] * 2 + [STATS, WIDE_KEYS, WIDE_GRADS],
    [SEQUENCE, SEQUENCE, on_lanes(2, BLOCK)],
    (shape_of(BF16, BLOCK, D), shape_of(BF16, BLOCK, D), shape_of(F32, 2, BLOCK, D)),
    [
        pltpu.VMEM((UNROLL, BLOCK, 2 * PAIR), BF16),
        pltpu.VMEM((UNROLL, BLOCK, BOTH), BF16),
    ],
)
collect = pl.pallas_call(
    collect_kernel,
    out_shape=(shape_of(F32, 2, OWN, D), shape_of(F32, 8, D)),
    compiler_params=pltpu.CompilerParams(vmem_limit_bytes=16 * 1024 * 1024),
    name="collect",
)
finish = call(
    finish_kernel,
    "finish",
    TILES,
    [on_middle(2, ROWS, D)]
    + [on_middle(2, ROWS // P1, D)] * 3
    + [every(2, OWN, D)] * 2
    + [every(8, D)] * 2,
    [on_rows(ROWS, D)] * 2,
    (shape_of(BF16, BLOCK, D), shape_of(BF16, BLOCK, D)),
    [pltpu.VMEM((2, OWN, D), F32)],
)


def shifted(block, distance):
    count = lax.axis_size(("grp", "seq"))
    route = [(i, i + distance) for i in range(count) if 0 <= i + distance < count]
    return lax.ppermute(block, ("grp", "seq"), route)


def grp_swap(block, bit):
    return lax.ppermute(block, "grp", [(i, i ^ bit) for i in range(4)])


def exchanged(payload):
    return lax.all_to_all(payload, "seq", 0, 0, tiled=True)


def per_device(queries, keys, values, out_grad):
    device = lax.axis_index("grp") * N_SEQ + lax.axis_index("seq")
    count = lax.axis_size(("grp", "seq"))
    live = jnp.stack(
        [jnp.where(device == 0, NEG, 0.0), jnp.where(device == count - 1, NEG, 0.0)]
    ).astype(F32)
    top, pooled, *payloads = group_summaries(keys, values)
    swapped = grp_swap(top, 2)
    near, near_pooled = near_summaries(keys, values)
    near, live = lax.optimization_barrier((near, live))
    payloads[0], near_pooled = lax.optimization_barrier((payloads[0], near_pooled))
    top_pair = jnp.stack([top, swapped], axis=1).reshape(8, D)
    for part in range(PARTS):
        tops = top_pair[:, part * LANES : part * LANES + LANES]
        payloads[part] = lax.dynamic_update_slice(
            payloads[part], jnp.broadcast_to(tops[None], (N_SEQ, 8, LANES)), (0, 2 * OWN, 0)
        )
    everyone = [exchanged(payloads[0])]
    before = shifted(near, 1)
    after = shifted(near, -1)
    diag_weights, diag_sum, diag_stats, grad_t = diag_forward(queries, keys, values, out_grad)
    payloads[1], everyone[0], diag_sum, before, after = lax.optimization_barrier(
        (payloads[1], everyone[0], diag_sum, before, after)
    )
    everyone.append(exchanged(payloads[1]))
    kept, returned = (), []
    for part in range(PARTS):
        if part:
            top_mine = everyone[part][:, 2 * OWN :]
            top_other, returned[-1] = lax.optimization_barrier(
                (grp_swap(top_mine, 1), returned[-1])
            )
            returned[-1] = exchanged(returned[-1])
        else:
            top_mine = everyone[part][:, 2 * OWN :]
            top_other = grp_swap(top_mine, 1)
        *kept, back, dmine, dother = wide_attend(
            part, live, queries, grad_t, before, after, diag_sum, diag_stats,
            everyone[part], top_mine, top_other, *kept,
        )
        if part:
            back, dmine, dother, returned[0] = lax.optimization_barrier(
                (back, dmine, dother, returned[0])
            )
        dmine = (dmine.astype(F32) + grp_swap(dother, 1).astype(F32)).astype(BF16)
        returned.append(lax.dynamic_update_slice(back, dmine, (0, 2 * OWN, 0)))
    returned[-1] = exchanged(returned[-1])
    out_t, scaled, delta, kcat, sgrad, dbefore, dafter = kept
    from_next = shifted(dbefore, -1)
    from_prev = shifted(dafter, 1)
    out, dq, diag = diag_backward(
        queries, keys, values, diag_weights, out_t, scaled, delta, kcat, sgrad
    )
    returned[-1], diag = lax.optimization_barrier((returned[-1], diag))
    group_up, top_up = collect(*returned)
    swapped = grp_swap(top_up, 2)
    dk, dv = finish(
        diag, near_pooled, from_prev, from_next, pooled, group_up, top_up, swapped
    )
    return out, dq, dk, dv


def solution(mesh):
    spec = P(("grp", "seq"), None)
    return jax.shard_map(
        per_device, mesh=mesh, in_specs=(spec,) * 4, out_specs=(spec,) * 4, check_vma=False
    )
```

```python
import functools
import math

import jax
import jax.numpy as jnp
from jax import lax
from jax.experimental import pallas as pl
from jax.experimental.pallas import tpu as pltpu
from jax.sharding import PartitionSpec as P

D = 1024
H = 16
HD = 64
PAIR = 2 * HD
PAIRS = D // PAIR
BLOCK = 512
BOTH = 2 * BLOCK
P1 = 4
P2 = 32
RATIO = 8
NEAR = BLOCK // P1
OWN = BLOCK // P2
N_SEQ = 32
GROUP = OWN * N_SEQ
TOP = 256
SENT = 2 * OWN + 8
WIDE = GROUP + TOP + 2 * NEAR
CHUNK = 256
ROWS = 128
TILES = BLOCK // ROWS
UNROLL = 2
PARTS = 2
LANES = D // PARTS
PART_STEPS = PAIRS // PARTS // UNROLL
LAG = 8
SOFT = 1.0 / math.sqrt(HD)

EPS = 1e-06
NEG = -1e30
LOG2E = math.log2(math.e)

F32 = jnp.float32
BF16 = jnp.bfloat16


def dot(a, b):
    return jnp.dot(a, b, preferred_element_type=F32)


def dot_rows(a, b):
    return lax.dot_general(a, b, (((1,), (1,)), ((), ())), preferred_element_type=F32)


def pieces(x, count):
    parts = []
    for _ in range(count):
        low = x.astype(BF16)
        parts.append(low)
        x = x - low.astype(F32)
    return parts


def pool_matrix(rows, cols, factor):
    row = lax.broadcasted_iota(jnp.int32, (rows, cols), 0)
    col = lax.broadcasted_iota(jnp.int32, (rows, cols), 1)
    return jnp.where(col // factor == row, 1.0, 0.0).astype(BF16)


def spread_matrix(rows, cols, factor):
    row = lax.broadcasted_iota(jnp.int32, (rows, cols), 0)
    col = lax.broadcasted_iota(jnp.int32, (rows, cols), 1)
    return jnp.where(row // factor == col, 1.0, 0.0).astype(BF16)


def head_means(count_pieces, *xs):
    width = 256
    row = lax.broadcasted_iota(jnp.int32, (width, width), 0)
    col = lax.broadcasted_iota(jnp.int32, (width, width), 1)
    same = jnp.where(row // HD == col // HD, 1.0 / HD, 0.0).astype(BF16)
    stack = [x[:, start : start + width] for x in xs for start in range(0, D, width)]
    stack = jnp.concatenate(stack, axis=0)
    count = stack.shape[0]
    found = dot(jnp.concatenate(pieces(stack, count_pieces), axis=0), same)
    found = sum(found[at : at + count] for at in range(0, count_pieces * count, count))
    means, at = [], 0
    for x in xs:
        rows = x.shape[0]
        tiles = [found[at + t * rows : at + t * rows + rows] for t in range(D // width)]
        means.append(jnp.concatenate(tiles, axis=1))
        at += rows * (D // width)
    return means


def normalize(*pooled):
    means = head_means(3, *[x * x for x in pooled])
    return [x * lax.rsqrt(mean + EPS) for x, mean in zip(pooled, means)]


def normalize_back(pooled, upstream):
    means = head_means(2, *[x * x for x in pooled], *[x * up for x, up in zip(pooled, upstream)])
    back = []
    for x, up, mean, inner in zip(pooled, upstream, means, means[len(pooled) :]):
        scale = lax.rsqrt(mean + EPS)
        back.append(scale * (up - x * (scale * scale * inner)))
    return back


def top_pool(rows):
    return jnp.mean(rows.astype(F32).reshape(rows.shape[0] // RATIO, RATIO, rows.shape[1]), axis=1)


def group_kernel(k_ref, v_ref, top_ref, pooled_ref, *rest):
    payloads, groups = rest[:PARTS], rest[PARTS]
    tile = pl.program_id(0)
    for index, ref in enumerate((k_ref, v_ref)):
        groups[index, tile] = dot(pool_matrix(8, ROWS, P2), ref[...]) * (1.0 / P2)

    @pl.when(tile == TILES - 1)
    def _():
        pooled = []
        for index in range(2):
            parts = [groups[index, t][: ROWS // P2] for t in range(TILES)]
            pooled.append(jnp.concatenate(parts, axis=0))
            pooled_ref[index] = pooled[index]
        low = [group.astype(BF16) for group in normalize(*pooled)]
        for index, group in enumerate(low):
            for part, payload_ref in enumerate(payloads):
                lanes = slice(part * LANES, part * LANES + LANES)
                payload_ref[:, index * OWN : index * OWN + OWN] = jnp.broadcast_to(
                    group[None, :, lanes], (N_SEQ, OWN, LANES)
                )
        for index, top in enumerate(normalize(*[top_pool(group) for group in low])):
            top_ref[index] = top.astype(BF16)


def near_kernel(k_ref, v_ref, near_ref, near_pooled_ref):
    pooled = []
    for index, ref in enumerate((k_ref, v_ref)):
        pooled.append(dot(pool_matrix(ROWS // P1, ROWS, P1), ref[...]) * (1.0 / P1))
        near_pooled_ref[index] = pooled[index]
    for index, near in enumerate(normalize(*pooled)):
        near_ref[index] = near.astype(BF16)


def collect_kernel(*refs):
    backs, (up_ref, top_ref) = refs[:PARTS], refs[PARTS:]
    for part, back_ref in enumerate(backs):
        lanes = slice(part * LANES, part * LANES + LANES)
        total = jnp.sum(back_ref[:, : 2 * OWN].astype(F32), axis=0)
        up_ref[:, :, lanes] = total.reshape(2, OWN, LANES)
        top_ref[:, lanes] = jnp.sum(back_ref[:, 2 * OWN :].astype(F32), axis=0)


def finish_kernel(
    diag_ref, near_pooled_ref, prev_ref, next_ref, pooled_ref, up_ref, top_ref, swapped_ref,
    dk_ref, dv_ref, spread,
):
    tile = pl.program_id(0)

    @pl.when(tile == 0)
    def _():
        pooled = [pooled_ref[0], pooled_ref[1]]
        tops = [top_pool(group.astype(BF16)) for group in normalize(*pooled)]
        top_up = [
            top_ref[4 * index : 4 * index + 2] + swapped_ref[4 * index + 2 : 4 * index + 4]
            for index in range(2)
        ]
        ups = []
        for index, back in enumerate(normalize_back(tops, top_up)):
            back = jnp.broadcast_to(back[:, None, :] * (1.0 / RATIO), (OWN // RATIO, RATIO, D))
            ups.append(up_ref[index] + back.reshape(OWN, D))
        for index, back in enumerate(normalize_back(pooled, ups)):
            spread[index] = back * (1.0 / P2)

    count = ROWS // P1
    near_up = [prev_ref[index].astype(F32) + next_ref[index].astype(F32) for index in range(2)]
    over = spread_matrix(ROWS, count, P1)
    over = jnp.concatenate([over, over], axis=1)
    near_back = normalize_back([near_pooled_ref[0], near_pooled_ref[1]], near_up)
    for index, out_ref in enumerate((dk_ref, dv_ref)):
        both = jnp.concatenate(pieces(near_back[index] * (1.0 / P1), 2), axis=0)
        total = diag_ref[index] + dot(over, both)
        for place in range(ROWS // P2):
            cut = slice(place * P2, place * P2 + P2)
            row = spread[index, pl.ds(tile * (ROWS // P2) + place, 1)]
            out_ref[cut] = (total[cut] + row).astype(BF16)


def starts(count):
    return range(0, count, CHUNK)


def apart(x_t):
    zero = jnp.zeros((HD, BLOCK), x_t.dtype)
    first = jnp.concatenate([x_t[:HD], zero], axis=1)
    second = jnp.concatenate([zero, x_t[HD:]], axis=1)
    return jnp.concatenate([first, second], axis=0)


def together(x):
    return jnp.concatenate([x[:HD, :BLOCK], x[HD:PAIR, BLOCK:]], axis=0)


def by_head(row):
    return jnp.concatenate(
        [jnp.broadcast_to(row[:, :BLOCK], (HD, BLOCK)), jnp.broadcast_to(row[:, BLOCK:], (HD, BLOCK))],
        axis=0,
    )


def head_sums(x):
    return jnp.concatenate(
        [jnp.sum(x[:HD], axis=0, keepdims=True), jnp.sum(x[HD:], axis=0, keepdims=True)], axis=1
    )


def head_rows(x):
    lane = lax.broadcasted_iota(jnp.int32, x.shape, 1)
    zero = jnp.zeros((), BF16)
    return jnp.concatenate([jnp.where(lane < HD, x, zero), jnp.where(lane < HD, zero, x)], axis=0)


def score_step(start, q_rows, kcat, scores, bias, largest):
    part = dot_rows(kcat[start : start + CHUNK], q_rows)
    if start in bias:
        part = part + bias[start]
    scores[start : start + CHUNK] = part
    part = jnp.max(part.reshape(CHUNK // 8, 8, BOTH), axis=0)
    return part if largest is None else jnp.maximum(largest, part)


def weight_step(start, scores, weights, largest):
    part = (scores[start : start + CHUNK] - largest) * (LOG2E * SOFT)
    weights[start : start + CHUNK] = jnp.exp2(part).astype(BF16)


def value_step(v_t, weights):
    found = dot(jnp.concatenate([v_t, jnp.ones((16, v_t.shape[1]), BF16)], axis=0), weights[...])
    return found[PAIR : PAIR + 1], together(found)


def grads_and_delta(scaled, delta):
    row = lax.broadcasted_iota(jnp.int32, (16, BOTH), 0)
    extra = jnp.zeros((16, BOTH), F32)
    for place, piece in enumerate(pieces(-delta, 3)):
        extra = jnp.where(row == place, piece.astype(F32), extra)
    zero = jnp.zeros((PAIR - 16, BOTH), BF16)
    return jnp.concatenate([apart(scaled), extra.astype(BF16), zero], axis=0)


def grad_step(start, g_both, vones, weights, sgrad):
    cut = slice(start, start + CHUNK)
    part = dot(vones[cut], g_both)
    sgrad[cut] = (part * weights[cut].astype(F32)).astype(BF16)


def pair_lanes():
    return [(p, slice(p * PAIR, p * PAIR + PAIR)) for p in range(UNROLL)]


def diag_kernel(q_ref, k_ref, v_ref, g_ref, weights_ref, sum_ref, stats_ref, g_t_ref, scores):
    running = [
        diag_pair(
            q_ref.at[:, lanes], k_ref.at[:, lanes], v_ref.at[:, lanes], g_ref.at[:, lanes],
            weights_ref.at[p], sum_ref.at[lanes], stats_ref.at[p], g_t_ref.at[lanes], scores.at[p],
        )
        for p, lanes in pair_lanes()
    ]
    staggered(running, BLOCK // CHUNK)


def diag_pair(q_ref, k_ref, v_ref, g_ref, weights, sum_ref, stats_ref, g_t_ref, scores):
    g_t_ref[...] = g_ref[...].T
    q_rows = head_rows(q_ref[...])
    largest = None
    for start in starts(BLOCK):
        largest = score_step(start, q_rows, k_ref, scores, {}, largest)
        yield True
    largest = jnp.max(largest, axis=0, keepdims=True)
    for start in starts(BLOCK):
        weight_step(start, scores, weights, largest)
        yield True
    total, summed = value_step(v_ref[...].T, weights)
    stats_ref[0:1] = largest
    stats_ref[1:2] = total
    sum_ref[...] = summed
    yield True


def low_rows(shape):
    return lax.broadcasted_iota(jnp.int32, shape, 1) < 4


def split_top(ref, lanes):
    both = ref[:, :, lanes].astype(F32).reshape(N_SEQ // 2, 2, 8, PAIR)
    first, second = both[:, 0], both[:, 1]
    low = low_rows(first.shape)
    k = jnp.where(low, first, pltpu.roll(second, 4, 1))
    v = jnp.where(low, pltpu.roll(first, 4, 1), second)
    return k.reshape(TOP // 2, PAIR).astype(BF16), v.reshape(TOP // 2, PAIR).astype(BF16)


def join_top(k, v):
    k = k.reshape(N_SEQ // 2, 8, PAIR)
    v = v.reshape(N_SEQ // 2, 8, PAIR)
    low = low_rows(k.shape)
    first = jnp.where(low, k, pltpu.roll(v, 4, 1))
    second = jnp.where(low, pltpu.roll(k, 4, 1), v)
    return jnp.stack([first, second], axis=1).reshape(N_SEQ, 8, PAIR).astype(BF16)


def wide_kernel(
    live_ref, q_ref, g_ref, before_ref, after_ref, sum_ref, stats_ref,
    group_ref, mine_ref, other_ref, *rest,
):
    (
        out_ref, scaled_ref, delta_ref, dq_ref, dbefore_ref, dafter_ref,
        dgroup_ref, dmine_ref, dother_ref, kcats, vones, scores, weights, sgrads,
    ) = rest[-14:]
    near_row = lax.broadcasted_iota(jnp.int32, (CHUNK, 1), 0)
    bias = {GROUP + TOP: jnp.where(near_row < NEAR, live_ref[0], live_ref[1])}

    @pl.when(pl.program_id(0) == 0)
    def _():
        vones[:, :, PAIR:] = jnp.ones((UNROLL, WIDE, PAIR), BF16)

    running = []
    for p in range(UNROLL):
        lanes = slice(p * PAIR, p * PAIR + PAIR)
        running.append(wide_pair(
            bias, q_ref.at[:, lanes], g_ref.at[lanes],
            before_ref.at[:, :, lanes], after_ref.at[:, :, lanes],
            sum_ref.at[lanes], stats_ref.at[p], group_ref.at[:, :, lanes],
            split_top(mine_ref, lanes), split_top(other_ref, lanes),
            out_ref.at[lanes], scaled_ref.at[lanes], delta_ref.at[p],
            dq_ref.at[lanes], kcats.at[p], sgrads.at[p],
            dgroup_ref.at[:, :, lanes], dmine_ref.at[:, :, lanes], dother_ref.at[:, :, lanes],
            dbefore_ref.at[:, :, lanes], dafter_ref.at[:, :, lanes],
            vones.at[p], scores.at[p], weights.at[p],
        ))
    staggered(running, LAG)


def staggered(running, lag):
    tick, left = 0, list(enumerate(running))
    while left:
        for item in list(left):
            index, steps = item
            if tick >= index * lag and next(steps, None) is None:
                left.remove(item)
        tick += 1


def wide_pair(
    bias, q_ref, g_ref, before_ref, after_ref, sum_ref, stats_ref, group_ref, mine, other,
    out_ref, scaled_ref, delta_ref, dq_ref, kcat, sgrad,
    dgroup_ref, dmine_ref, dother_ref, dbefore_ref, dafter_ref,
    vones, scores, weights,
):
    kcat[0:GROUP] = group_ref[:, 0:OWN].reshape(GROUP, PAIR)
    vones[0:GROUP, :PAIR] = group_ref[:, OWN : 2 * OWN].reshape(GROUP, PAIR)
    for start, (k, v) in ((GROUP, mine), (GROUP + TOP // 2, other)):
        kcat[start : start + TOP // 2] = k
        vones[start : start + TOP // 2, :PAIR] = v
    for start, ref in ((GROUP + TOP, before_ref), (GROUP + TOP + NEAR, after_ref)):
        kcat[start : start + NEAR] = ref[0]
        vones[start : start + NEAR, :PAIR] = ref[1]
    q_rows = head_rows(q_ref[...])
    largest = None
    for start in starts(WIDE):
        largest = score_step(start, q_rows, kcat, scores, bias, largest)
        yield True
    largest = jnp.max(largest, axis=0, keepdims=True)
    for start in starts(WIDE):
        weight_step(start, scores, weights, largest)
        yield True
    total, summed = value_step(vones[:, :PAIR].T, weights)
    yield True
    local_largest, local_total = stats_ref[0:1], stats_ref[1:2]
    most = jnp.maximum(largest, local_largest)
    share = jnp.exp2((largest - most) * (LOG2E * SOFT))
    local_share = jnp.exp2((local_largest - most) * (LOG2E * SOFT))
    inverse = 1.0 / (share * total + local_share * local_total)
    share = by_head(share * inverse)
    local_share = by_head(local_share * inverse)
    attended = share * summed + local_share * sum_ref[...]
    out_ref[...] = attended.astype(BF16)
    grad = g_ref[...].astype(F32)
    local_scaled = (grad * local_share).astype(BF16)
    scaled_ref[...] = local_scaled
    delta_ref[0:1] = head_sums(local_scaled.astype(F32) * attended)
    scaled = (grad * share).astype(BF16)
    g_both = grads_and_delta(scaled, head_sums(scaled.astype(F32) * attended))
    yield True
    for start in starts(WIDE):
        grad_step(start, g_both, vones, weights, sgrad)
        yield True
    dq_ref[...] = together(dot(kcat[...].T, sgrad[...]))
    yield True
    g_rows = head_rows(scaled.T)
    for start in starts(WIDE):
        cut = slice(start, start + CHUNK)
        dk = dot(sgrad[cut], q_rows) * SOFT
        dv = dot(weights[cut], g_rows)
        if start < GROUP:
            devices = slice(start // OWN, (start + CHUNK) // OWN)
            shape = (CHUNK // OWN, OWN, PAIR)
            dgroup_ref[devices, 0:OWN] = dk.astype(BF16).reshape(shape)
            dgroup_ref[devices, OWN : 2 * OWN] = dv.astype(BF16).reshape(shape)
        elif start < GROUP + TOP:
            half = TOP // 2
            dmine_ref[...] = join_top(dk[:half], dv[:half])
            dother_ref[...] = join_top(dk[half:], dv[half:])
        else:
            for index, value in enumerate((dk, dv)):
                dbefore_ref[index] = value[:NEAR].astype(BF16)
                dafter_ref[index] = value[NEAR:].astype(BF16)
        yield True


def diag_back_kernel(
    q_ref, k_ref, v_ref, weights_ref, out_t_ref, scaled_ref, delta_ref, wide_ref,
    out_ref, dq_ref, diag_ref, vones, sgrad,
):
    @pl.when(pl.program_id(0) == 0)
    def _():
        vones[:, :, PAIR:] = jnp.ones((UNROLL, BLOCK, PAIR), BF16)

    running = [
        diag_back_pair(
            q_ref.at[:, lanes], k_ref.at[:, lanes], v_ref.at[:, lanes], weights_ref.at[p],
            out_t_ref.at[lanes], scaled_ref.at[lanes], delta_ref.at[p],
            wide_ref.at[lanes], out_ref.at[:, lanes], dq_ref.at[:, lanes], diag_ref.at[:, :, lanes],
            vones.at[p], sgrad.at[p],
        )
        for p, lanes in pair_lanes()
    ]
    staggered(running, BLOCK // CHUNK)


def diag_back_pair(
    q_ref, k_ref, v_ref, weights, out_t_ref, scaled_ref, delta_ref, wide_ref,
    out_ref, dq_ref, diag_ref, vones, sgrad,
):
    vones[:, :PAIR] = v_ref[...]
    out_ref[...] = out_t_ref[...].T
    scaled = scaled_ref[...]
    g_both = grads_and_delta(scaled, delta_ref[0:1])
    for start in starts(BLOCK):
        grad_step(start, g_both, vones, weights, sgrad)
        yield True
    dq = wide_ref[...] + together(dot(k_ref[...].T, sgrad[...]))
    dq_ref[...] = (dq.T * SOFT).astype(BF16)
    yield True
    q_rows = head_rows(q_ref[...])
    g_rows = head_rows(scaled.T)
    for start in starts(BLOCK):
        cut = slice(start, start + CHUNK)
        diag_ref[0, cut] = dot(sgrad[cut], q_rows) * SOFT
        diag_ref[1, cut] = dot(weights[cut], g_rows)
        yield True


def shape_of(dtype, *shape):
    return jax.ShapeDtypeStruct(shape, dtype)


def on_lanes(*lead):
    return pl.BlockSpec(lead + (UNROLL * PAIR,), lambda p: (0,) * len(lead) + (p,))


def on_rows(*shape):
    return pl.BlockSpec(shape, lambda p: (p,) + (0,) * (len(shape) - 1))


def on_middle(*shape):
    return pl.BlockSpec(shape, lambda p: (0, p, 0))


def every(*shape):
    return pl.BlockSpec(shape, lambda p: (0,) * len(shape))


SMEM = pl.BlockSpec(memory_space=pltpu.SMEM)
SEQUENCE = on_lanes(BLOCK)
COLUMNS = on_rows(UNROLL * PAIR, BLOCK)
STATS = on_rows(UNROLL, 8, BOTH)
DIAG = on_rows(UNROLL, BLOCK, BOTH)


def call(kernel, name, steps, in_specs, out_specs, out_shape, scratch=()):
    return pl.pallas_call(
        kernel,
        grid=(steps,),
        in_specs=in_specs,
        out_specs=out_specs,
        out_shape=out_shape,
        scratch_shapes=scratch,
        compiler_params=pltpu.CompilerParams(vmem_limit_bytes=56 * 1024 * 1024),
        name=name,
    )


group_summaries = call(
    group_kernel,
    "group_summaries",
    TILES,
    [on_rows(ROWS, D)] * 2,
    [every(2, OWN // RATIO, D), every(2, OWN, D)] + [every(N_SEQ, 2 * OWN, LANES)] * PARTS,
    (shape_of(BF16, 2, OWN // RATIO, D), shape_of(F32, 2, OWN, D))
    + (shape_of(BF16, N_SEQ, SENT, LANES),) * PARTS,
    [pltpu.VMEM((2, TILES, 8, D), F32)],
)
near_summaries = call(
    near_kernel,
    "near_summaries",
    TILES,
    [on_rows(ROWS, D)] * 2,
    [on_middle(2, ROWS // P1, D)] * 2,
    (shape_of(BF16, 2, NEAR, D), shape_of(F32, 2, NEAR, D)),
)
diag_forward = call(
    diag_kernel,
    "diag_forward",
    PAIRS // UNROLL,
    [SEQUENCE] * 4,
    [DIAG, COLUMNS, STATS, COLUMNS],
    (
        shape_of(BF16, PAIRS, BLOCK, BOTH),
        shape_of(F32, D, BLOCK),
        shape_of(F32, PAIRS, 8, BOTH),
        shape_of(BF16, D, BLOCK),
    ),
    [pltpu.VMEM((UNROLL, BLOCK, BOTH), F32)],
)
def wide_attend(part, *args):
    offset = part * PART_STEPS

    def part_lanes(*lead):
        return pl.BlockSpec(lead + (UNROLL * PAIR,), lambda p: (0,) * len(lead) + (p,))

    def wide_lanes(*lead):
        return pl.BlockSpec(
            lead + (UNROLL * PAIR,), lambda p: (0,) * len(lead) + (p + offset,)
        )

    def wide_rows(*shape):
        return pl.BlockSpec(shape, lambda p: (p + offset,) + (0,) * (len(shape) - 1))

    in_specs = (
        [SMEM, wide_lanes(BLOCK), wide_rows(UNROLL * PAIR, BLOCK)]
        + [wide_lanes(2, NEAR)] * 2
        + [wide_rows(UNROLL * PAIR, BLOCK), wide_rows(UNROLL, 8, BOTH)]
        + [part_lanes(N_SEQ, 2 * OWN)]
        + [part_lanes(N_SEQ, 8)] * 2
    )
    shared = len(args) - len(in_specs)
    aliases = {len(in_specs) + index: index for index in range(shared)}
    return pl.pallas_call(
        wide_kernel,
        grid=(PART_STEPS,),
        in_specs=in_specs + [pl.BlockSpec(memory_space=pl.ANY)] * shared,
        out_specs=[wide_rows(UNROLL * PAIR, BLOCK)] * 2
        + [wide_rows(UNROLL, 8, BOTH), wide_rows(UNROLL * PAIR, BLOCK)]
        + [wide_lanes(2, NEAR)] * 2
        + [part_lanes(N_SEQ, 2 * OWN)]
        + [part_lanes(N_SEQ, 8)] * 2,
        out_shape=(
            shape_of(BF16, D, BLOCK),
            shape_of(BF16, D, BLOCK),
            shape_of(F32, PAIRS, 8, BOTH),
            shape_of(F32, D, BLOCK),
            shape_of(BF16, 2, NEAR, D),
            shape_of(BF16, 2, NEAR, D),
            shape_of(BF16, N_SEQ, SENT, LANES),
            shape_of(BF16, N_SEQ, 8, LANES),
            shape_of(BF16, N_SEQ, 8, LANES),
        ),
        scratch_shapes=[
            pltpu.VMEM((UNROLL, WIDE, PAIR), BF16),
            pltpu.VMEM((UNROLL, WIDE, 2 * PAIR), BF16),
            pltpu.VMEM((UNROLL, WIDE, BOTH), F32),
            pltpu.VMEM((UNROLL, WIDE, BOTH), BF16),
            pltpu.VMEM((UNROLL, WIDE, BOTH), BF16),
        ],
        input_output_aliases=aliases,
        compiler_params=pltpu.CompilerParams(vmem_limit_bytes=56 * 1024 * 1024),
        name="wide_attend%d" % part,
    )(*args)


diag_backward = call(
    diag_back_kernel,
    "diag_backward",
    PAIRS // UNROLL,
    [SEQUENCE] * 3 + [DIAG] + [COLUMNS] * 2 + [STATS, COLUMNS],
    [SEQUENCE, SEQUENCE, on_lanes(2, BLOCK)],
    (shape_of(BF16, BLOCK, D), shape_of(BF16, BLOCK, D), shape_of(F32, 2, BLOCK, D)),
    [
        pltpu.VMEM((UNROLL, BLOCK, 2 * PAIR), BF16),
        pltpu.VMEM((UNROLL, BLOCK, BOTH), BF16),
    ],
)
collect = pl.pallas_call(
    collect_kernel,
    out_shape=(shape_of(F32, 2, OWN, D), shape_of(F32, 8, D)),
    compiler_params=pltpu.CompilerParams(vmem_limit_bytes=16 * 1024 * 1024),
    name="collect",
)
finish = call(
    finish_kernel,
    "finish",
    TILES,
    [on_middle(2, ROWS, D)]
    + [on_middle(2, ROWS // P1, D)] * 3
    + [every(2, OWN, D)] * 2
    + [every(8, D)] * 2,
    [on_rows(ROWS, D)] * 2,
    (shape_of(BF16, BLOCK, D), shape_of(BF16, BLOCK, D)),
    [pltpu.VMEM((2, OWN, D), F32)],
)


def shifted(block, distance):
    count = lax.axis_size(("grp", "seq"))
    route = [(i, i + distance) for i in range(count) if 0 <= i + distance < count]
    return lax.ppermute(block, ("grp", "seq"), route)


def grp_swap(block, bit):
    return lax.ppermute(block, "grp", [(i, i ^ bit) for i in range(4)])


def exchanged(payload):
    return lax.all_to_all(payload, "seq", 0, 0, tiled=True)


def per_device(queries, keys, values, out_grad):
    device = lax.axis_index("grp") * N_SEQ + lax.axis_index("seq")
    count = lax.axis_size(("grp", "seq"))
    live = jnp.stack(
        [jnp.where(device == 0, NEG, 0.0), jnp.where(device == count - 1, NEG, 0.0)]
    ).astype(F32)
    top, pooled, *payloads = group_summaries(keys, values)
    swapped = grp_swap(top, 2)
    near, near_pooled = near_summaries(keys, values)
    near, live = lax.optimization_barrier((near, live))
    payloads[0], near_pooled = lax.optimization_barrier((payloads[0], near_pooled))
    top_pair = jnp.stack([top, swapped], axis=1).reshape(8, D)
    for part in range(PARTS):
        tops = top_pair[:, part * LANES : part * LANES + LANES]
        payloads[part] = lax.dynamic_update_slice(
            payloads[part], jnp.broadcast_to(tops[None], (N_SEQ, 8, LANES)), (0, 2 * OWN, 0)
        )
    everyone = [exchanged(payloads[0])]
    before = shifted(near, 1)
    after = shifted(near, -1)
    diag_weights, diag_sum, diag_stats, grad_t = diag_forward(queries, keys, values, out_grad)
    payloads[1], everyone[0], diag_sum, before, after = lax.optimization_barrier(
        (payloads[1], everyone[0], diag_sum, before, after)
    )
    everyone.append(exchanged(payloads[1]))
    kept, returned = (), []
    for part in range(PARTS):
        if part:
            top_mine = everyone[part][:, 2 * OWN :]
            top_other, returned[-1] = lax.optimization_barrier(
                (grp_swap(top_mine, 1), returned[-1])
            )
            returned[-1] = exchanged(returned[-1])
        else:
            top_mine = everyone[part][:, 2 * OWN :]
            top_other = grp_swap(top_mine, 1)
        *kept, back, dmine, dother = wide_attend(
            part, live, queries, grad_t, before, after, diag_sum, diag_stats,
            everyone[part], top_mine, top_other, *kept,
        )
        if part:
            back, dmine, dother, returned[0] = lax.optimization_barrier(
                (back, dmine, dother, returned[0])
            )
        dmine = (dmine.astype(F32) + grp_swap(dother, 1).astype(F32)).astype(BF16)
        returned.append(lax.dynamic_update_slice(back, dmine, (0, 2 * OWN, 0)))
    returned[-1] = exchanged(returned[-1])
    out_t, scaled, delta, dq_t, dbefore, dafter = kept
    from_next = shifted(dbefore, -1)
    from_prev = shifted(dafter, 1)
    out, dq, diag = diag_backward(
        queries, keys, values, diag_weights, out_t, scaled, delta, dq_t
    )
    returned[-1], diag = lax.optimization_barrier((returned[-1], diag))
    group_up, top_up = collect(*returned)
    swapped = grp_swap(top_up, 2)
    dk, dv = finish(
        diag, near_pooled, from_prev, from_next, pooled, group_up, top_up, swapped
    )
    return out, dq, dk, dv


def solution(mesh):
    spec = P(("grp", "seq"), None)
    return jax.shard_map(
        per_device, mesh=mesh, in_specs=(spec,) * 4, out_specs=(spec,) * 4, check_vma=False
    )
```
